256 devices in a mesh: seq: 32 (over y_hi, z, core), grp: 8 (over x, y_lo).
Axes of the slice: x: 4, y: 4 (y_hi: 2, y_lo: 2; y = y_hi * 2 + y_lo), z: 8, core: 2. Of those that a mesh axis runs over, the one named last changes fastest.
Arguments:
- units: bfloat16 [32768, 1024], P(('grp', 'seq')), parts along dimension 0, may hold values from -6 to 6
- durations: int32 [32768], P(('grp', 'seq')), parts along dimension 0, may hold values from 1 to 12, 24576 in all
- seg_ids: int32 [32768], P(('grp', 'seq')), parts along dimension 0, may hold values from 0 to 7, never falling along the last dimension, each value on 1 to 2048 neighbouring positions
- ln_gain: float32 [1024], replicated, may hold values from 0.1 to 1.9
- w_qkv: bfloat16 [1024, 3072], replicated, may hold values from -8 to 8
- w_out: bfloat16 [1024, 1024], replicated, may hold values from -0.1875 to 0.1875
- w_proj: bfloat16 [1024, 512], replicated, may hold values from -0.1875 to 0.1875
- conv_w: bfloat16 [5, 512, 512], replicated, may hold values from -0.125 to 0.125
- conv_b: float32 [512], replicated, may hold values from -3 to 3
- conv_gain: float32 [512], replicated, may hold values from 0.1 to 1.9
Outputs:
- frames_out: bfloat16 [196608, 512], P(('grp', 'seq')), parts along dimension 0
The draws below stay inside these ranges and needn't reach their ends.
There are 8 independent parts, one for each index of `grp`. The reference program is written for one: setup_inputs(seed, part) draws one part's arguments, and reference() takes and returns one part's arrays. A program takes and returns all parts, laid end to end along the dimension named above; an argument that names none is the same for every part. Nothing has to cross between parts.
All inputs are finite; a program needn't handle non-finite values. No bound on the sum of `durations` on one device may be relied on, other than what follows from the above.
Results may differ from the reference program's by a relative error of at most 0.0098.
Values may be sent and summed in bfloat16 or wider, within the bound.
A program may use at most 128 MiB of HBM per device.

```python
import math
import jax
import jax.numpy as jnp
import numpy as np
from jax import lax

D = 1024
HEADS = 16
C = 512
KERNEL = 5
SEGS = 8
UNITS = 4096
FRAMES = 24576


def draw_units(key, part):
    base = jax.random.truncated_normal(key, -6.0, 6.0, (UNITS, D), jnp.float32)
    return base.astype(jnp.bfloat16)


def draw_w_qkv(key, part):
    matrix = jax.random.truncated_normal(key, -6.0, 6.0, (D, 3 * D), jnp.float32) / math.sqrt(D)
    query_part = 3.0 * matrix[:, :D]
    key_part = 1.5 * matrix[:, D:2 * D]
    return jnp.concatenate([query_part, key_part, matrix[:, 2 * D:]], axis=1).astype(jnp.bfloat16)


def length_profile(number_of, total, reach, slope):
    weights = [(1 << 20) // math.isqrt(rank ** slope) + 1 for rank in range(2, number_of + 1)]
    surplus, counts = total - reach - (number_of - 1), [1] * (number_of - 1)
    while surplus > 0:
        free = [i for i in range(number_of - 1) if counts[i] < reach]
        mass, remaining = sum([weights[i] for i in free]), surplus
        for i in free:
            addition = min(reach - counts[i], max(1, remaining * weights[i] // mass), surplus)
            counts[i] = counts[i] + addition
            surplus = surplus - addition
    return np.array([reach] + counts)


def ragged_sizes(own_key, number_of, total, reach, skew):
    if number_of == 2:
        one = jax.random.randint(own_key, (), max(1, total - reach), min(reach, total - 1) + 1)
        return jnp.stack([one, total - one])
    lengths = jnp.asarray(length_profile(number_of, total, reach, skew), jnp.int32)
    pairs = (number_of - 1) // 2
    giver, taker = lengths[1:1 + 2 * pairs:2], lengths[2:2 + 2 * pairs:2]
    margin = jnp.minimum(giver - 1, reach - taker)
    shifted = jax.random.randint(jax.random.fold_in(own_key, 1), (pairs,), 0, 1 << 20) % (margin + 1)
    lengths = lengths.at[1:1 + 2 * pairs:2].set(giver - shifted).at[2:2 + 2 * pairs:2].set(taker + shifted)
    return lengths[jax.random.permutation(jax.random.fold_in(own_key, 2), number_of)]


def gaussian(stream_key, extent, width, bound, kind=jnp.bfloat16):
    values = width * jax.random.normal(stream_key, extent, jnp.float32)
    return jnp.clip(values, min=-bound, max=bound).astype(kind)


def setup_inputs(seed: int = 0, part: int = 0) -> dict:
    seeds = jax.random.split(jax.random.key(seed), 11)
    part_keys = jax.random.split(jax.random.fold_in(seeds[10], part), 11)
    units = draw_units(jax.random.fold_in(jax.random.fold_in(seeds[10], part), 71), part)
    durations = ragged_sizes(part_keys[1], UNITS, FRAMES, 12, 2).astype(jnp.int32)
    seg_ids = jnp.searchsorted(jnp.cumsum(ragged_sizes(part_keys[2], SEGS, UNITS, UNITS // 2, 0)), jnp.arange(UNITS), side="right").astype(jnp.int32)
    ln_gain = jnp.clip(1.0 + 0.18 * jax.random.normal(seeds[3], (D,), jnp.float32), 0.1, 1.9)
    w_qkv = draw_w_qkv(jax.random.fold_in(seeds[10], 71), part)
    w_out = gaussian(seeds[5], (D, D), D ** -0.5, 0.1875)
    w_proj = gaussian(seeds[6], (D, C), D ** -0.5, 0.1875)
    conv_w = gaussian(seeds[7], (KERNEL, C, C), (KERNEL * C) ** -0.5, 0.125)
    conv_b = gaussian(seeds[8], (C,), 0.5, 3.0, jnp.float32)
    conv_gain = jnp.clip(1.0 + 0.18 * jax.random.normal(seeds[9], (C,), jnp.float32), 0.1, 1.9)
    return {"units": units, "durations": durations, "seg_ids": seg_ids, "ln_gain": ln_gain, "w_qkv": w_qkv, "w_out": w_out, "w_proj": w_proj, "conv_w": conv_w, "conv_b": conv_b, "conv_gain": conv_gain}


def normalize(values, gain):
    mean = lax.optimization_barrier(jnp.mean(values, axis=-1, keepdims=True))
    centred = values - mean
    variance = lax.optimization_barrier(jnp.mean(centred * centred, axis=-1, keepdims=True))
    return centred / jnp.sqrt(variance + 1e-05) * gain

def reference(units, durations, seg_ids, ln_gain, w_qkv, w_out, w_proj, conv_w, conv_b, conv_gain):
    head_size = D // HEADS
    x = units.astype(jnp.float32)
    h = normalize(x, ln_gain).astype(jnp.bfloat16)
    qkv = jnp.dot(h, w_qkv, preferred_element_type=jnp.float32).astype(jnp.bfloat16)
    query = qkv[:, :D].reshape(UNITS, HEADS, head_size).transpose(1, 0, 2)
    keys = qkv[:, D:2 * D].reshape(UNITS, HEADS, head_size).transpose(1, 0, 2)
    values = qkv[:, 2 * D:].reshape(UNITS, HEADS, head_size).transpose(1, 0, 2)
    allowed = seg_ids[:, None] == seg_ids[None, :]
    scale = 1.0 / jnp.sqrt(jnp.float32(head_size))

    def one_head(parts):
        q_head, k_head, v_head = parts
        scores = jnp.dot(q_head, k_head.T, preferred_element_type=jnp.float32) * scale
        scores = jnp.where(allowed, scores, jnp.float32(-1e+30))
        top = lax.optimization_barrier(jnp.max(scores, axis=1, keepdims=True))
        expo = jnp.where(allowed, jnp.exp(scores - top), jnp.float32(0.0))
        total = lax.optimization_barrier(jnp.sum(expo, axis=1, keepdims=True))
        summed = jnp.dot(expo.astype(jnp.bfloat16), v_head, preferred_element_type=jnp.float32)
        return summed / total
    heads_out = lax.map(one_head, (query, keys, values))
    attended = heads_out.transpose(1, 0, 2).reshape(UNITS, D).astype(jnp.bfloat16)
    mixed = (jnp.dot(attended, w_out, preferred_element_type=jnp.float32) + x).astype(jnp.bfloat16)
    reduced = jnp.dot(mixed, w_proj, preferred_element_type=jnp.float32).astype(jnp.bfloat16)
    ends = jnp.cumsum(durations).astype(jnp.int32)
    frame_pos = jnp.arange(FRAMES, dtype=jnp.int32)
    unit_of = jnp.searchsorted(ends, frame_pos, side='right').astype(jnp.int32)
    expanded = jnp.take(reduced, unit_of, axis=0)
    half = KERNEL // 2
    padded = jnp.pad(expanded, ((half, half), (0, 0)))
    conv = jnp.zeros((FRAMES, C), jnp.float32) + conv_b
    for tap in range(KERNEL):
        conv = conv + jnp.dot(padded[tap:tap + FRAMES], conv_w[tap], preferred_element_type=jnp.float32)
    result = expanded.astype(jnp.float32) + normalize(jax.nn.relu(conv), conv_gain)
    return result.astype(jnp.bfloat16)
```

```python
import functools

import jax
import jax.numpy as jnp
from jax import lax
from jax.experimental import pallas as pl
from jax.experimental.pallas import tpu as pltpu
from jax.sharding import PartitionSpec as P

MESH = pl.DeviceIdType.MESH
SEQ = 32
CHIPS = 16
HEADS = 16
HEAD = 64
ROWS = 128
WIDTH = 1024
UNITS = 4096
CHANNELS = 512
KERNEL = 5
FRAMES = 768
STEP = 96
STEPS = FRAMES // STEP
KEYS = 512
NEG = -1e30
VMEM_LIMIT = 60 * 1024 * 1024


def seq(index):
    return {"seq": index}


def greet_all(me):
    barrier = pltpu.get_barrier_semaphore()

    def greet(i, carry):
        pl.semaphore_signal(
            barrier, 1, device_id=seq(lax.rem(me + i, SEQ)), device_id_type=MESH
        )
        return carry

    lax.fori_loop(1, SEQ, greet, 0)


def await_all():
    pl.semaphore_wait(pltpu.get_barrier_semaphore(), SEQ - 1)


def group_at(own, i):
    flip = own + 1 - 2 * lax.rem(own, 2)
    if i == 0:
        return flip
    if i == 1:
        return lax.rem(flip + 2, 4)
    if i == 2:
        return lax.rem(own + 2, 4)
    return own


def low_lanes(rows):
    return lax.broadcasted_iota(jnp.int32, (rows, 128), 1) < HEAD


def spread_kernel(
    units_ref,
    gain_ref,
    meta_ref,
    w_ref,
    kv_ref,
    q_ref,
    seg_ref,
    start_ref,
    end_ref,
    range_ref,
    h_ref,
    wbuf,
    send_kv,
    send_q,
    meta_all,
    w_sem,
    kv_send,
    kv_recv,
    q_send,
    q_recv,
    pass_send,
    pass_recv,
    meta_send,
    meta_recv,
    own_sem,
):
    me = lax.axis_index("seq")
    core = lax.rem(me, 2)
    chip = me // 2
    sibling = me + 1 - 2 * core
    own = chip // 4
    greet_all(me)

    def w_copy(i, t):
        g = group_at(own, i)
        return pltpu.make_async_copy(
            w_ref.at[:, pl.ds(t * WIDTH + g * 256, 256)], wbuf.at[i, t], w_sem.at[i, t]
        )

    for i in range(4):
        for t in range(3):
            w_copy(i, t).start()

    x = units_ref[...].astype(jnp.float32)
    mean = jnp.mean(x, axis=-1, keepdims=True)
    centred = x - mean
    variance = jnp.mean(centred * centred, axis=-1, keepdims=True)
    h_ref[...] = (centred / jnp.sqrt(variance + 1e-05) * gain_ref[...]).astype(jnp.bfloat16)

    await_all()

    def meta_copy(i, source):
        return pltpu.make_async_remote_copy(
            src_ref=meta_ref,
            dst_ref=meta_all.at[source],
            send_sem=meta_send.at[i],
            recv_sem=meta_recv.at[source],
            device_id=seq(lax.rem(me + i, SEQ)),
            device_id_type=MESH,
        )

    def send_meta(i, carry):
        meta_copy(i, me).start()
        return carry

    lax.fori_loop(1, SEQ, send_meta, 0)
    own_meta = pltpu.make_async_copy(meta_ref, meta_all.at[me], own_sem.at[2])
    own_meta.start()

    def kv_copy(head, source):
        return pltpu.make_async_remote_copy(
            src_ref=send_kv.at[head],
            dst_ref=kv_ref.at[2 * source + core],
            send_sem=kv_send.at[head],
            recv_sem=kv_recv.at[source],
            device_id=seq(2 * head + core),
            device_id_type=MESH,
        )

    def q_copy(head, source):
        return pltpu.make_async_remote_copy(
            src_ref=send_q.at[head],
            dst_ref=q_ref.at[source],
            send_sem=q_send.at[head],
            recv_sem=q_recv.at[source],
            device_id=seq(2 * head + core),
            device_id_type=MESH,
        )

    own_kv = pltpu.make_async_copy(send_kv.at[chip], kv_ref.at[me], own_sem.at[0])
    own_q = pltpu.make_async_copy(send_q.at[chip], q_ref.at[chip], own_sem.at[1])
    own_pass = pltpu.make_async_remote_copy(
        src_ref=send_kv.at[chip],
        dst_ref=kv_ref.at[me],
        send_sem=pass_send.at[chip],
        recv_sem=pass_recv.at[chip],
        device_id=seq(sibling),
        device_id_type=MESH,
    )

    low = low_lanes(ROWS)
    low_half = low_lanes(ROWS // 2)
    for i in range(4):
        g = group_at(own, i)
        for t in range(3):
            w_copy(i, t).wait()
        h = h_ref[...]
        q4, k4, v4 = (
            jnp.dot(h, wbuf[i, t], preferred_element_type=jnp.float32) for t in range(3)
        )
        for j in range(2):
            at = slice(128 * j, 128 * j + 128)
            q2, k2, v2 = q4[:, at] * 0.125, k4[:, at], v4[:, at]
            v_turned, k_turned = pltpu.roll(v2, HEAD, 1), pltpu.roll(k2, HEAD, 1)
            q_turned = pltpu.roll(q2, HEAD, 1)
            first = 4 * g + 2 * j
            send_kv[first] = jnp.where(low, k2, v_turned).astype(jnp.bfloat16)
            send_kv[first + 1] = jnp.where(low, k_turned, v2).astype(jnp.bfloat16)
            send_q[first] = jnp.where(low_half, q2[:64], q_turned[64:]).astype(jnp.bfloat16)
            send_q[first + 1] = jnp.where(low_half, q_turned[:64], q2[64:]).astype(jnp.bfloat16)
        for r in range(4):
            head = 4 * g + lax.rem(chip + r, 4)
            if i < 3:
                kv_copy(head, chip).start()
                q_copy(head, chip).start()
            elif r == 0:
                own_kv.start()
                own_pass.start()
                own_q.start()
            else:
                kv_copy(head, chip).start()
                q_copy(head, chip).start()

    def await_meta(i, carry):
        meta_copy(i, lax.rem(me + SEQ - i, SEQ)).wait()
        return carry

    lax.fori_loop(1, SEQ, await_meta, 0)
    own_meta.wait()

    seg = meta_all[:, 0, :]
    dur = meta_all[:, 1, :].astype(jnp.float32)
    lower = (
        lax.broadcasted_iota(jnp.int32, (128, 128), 0)
        <= lax.broadcasted_iota(jnp.int32, (128, 128), 1)
    ).astype(jnp.float32).astype(jnp.bfloat16)
    earlier = (
        lax.broadcasted_iota(jnp.int32, (SEQ, SEQ), 0)
        > lax.broadcasted_iota(jnp.int32, (SEQ, SEQ), 1)
    ).astype(jnp.float32).astype(jnp.bfloat16)
    dur16 = dur.astype(jnp.bfloat16)
    within = jnp.dot(dur16, lower, preferred_element_type=jnp.float32)
    before = jnp.dot(earlier, dur16, preferred_element_type=jnp.float32)
    ends = within + jnp.sum(before, axis=1, keepdims=True)
    seg_ref[...] = seg
    start_ref[...] = (ends - dur).astype(jnp.int32)
    end_ref[...] = ends.astype(jnp.int32)

    first_seg, last_seg = seg[:, 0:1], seg[:, 127:128]
    lane = lax.broadcasted_iota(jnp.int32, (SEQ, 128), 1)
    lo = jnp.zeros((SEQ, 1), jnp.int32)
    hi = jnp.zeros((SEQ, 1), jnp.int32)
    for s in range(8):
        below = jnp.sum((seg < s).astype(jnp.float32)).astype(jnp.int32)
        upto = jnp.sum((seg <= s).astype(jnp.float32)).astype(jnp.int32)
        lo = jnp.where(first_seg == s, below, lo)
        hi = jnp.where(last_seg == s, upto, hi)
    range_ref[0:SEQ, :] = jnp.where(lane == 0, lo, jnp.where(lane == 1, hi, 0))
    lane8 = lax.broadcasted_iota(jnp.int32, (8, 128), 1)
    block = jnp.zeros((8, 128), jnp.int32)
    for f in range(STEPS):
        t0 = (FRAMES * me + STEP * f - KERNEL // 2).astype(jnp.float32)
        passed = jnp.sum((ends <= t0).astype(jnp.float32)).astype(jnp.int32)
        block = jnp.where(lane8 == f, passed, block)
    range_ref[SEQ:, :] = block

    def passing(source):
        return pltpu.make_async_remote_copy(
            src_ref=kv_ref.at[2 * source + core],
            dst_ref=kv_ref.at[2 * source + core],
            send_sem=pass_send.at[source],
            recv_sem=pass_recv.at[source],
            device_id=seq(sibling),
            device_id_type=MESH,
        )

    for i in range(4):
        for r in range(4):
            if i == 3 and r == 0:
                continue
            source = 4 * group_at(own, i) + lax.rem(chip + 4 - r, 4)
            kv_copy(source, source).wait_recv()
            passing(source).start()

    for i in range(4):
        for r in range(4):
            source = 4 * group_at(own, i) + lax.rem(chip + 4 - r, 4)
            if i == 3 and r == 0:
                own_kv.wait()
                own_q.wait()
                own_pass.wait()
            else:
                q_copy(source, source).wait()
                kv_copy(source, source).wait_send()
                passing(source).wait()


def spread(units, gain, meta, w_qkv):
    any_space = pl.BlockSpec(memory_space=pl.ANY)
    vmem = pl.BlockSpec(memory_space=pltpu.VMEM)
    dma = pltpu.SemaphoreType.DMA
    return pl.pallas_call(
        spread_kernel,
        out_shape=(
            jax.ShapeDtypeStruct((SEQ, ROWS, 128), jnp.bfloat16),
            jax.ShapeDtypeStruct((CHIPS, ROWS // 2, 128), jnp.bfloat16),
            jax.ShapeDtypeStruct((SEQ, 128), jnp.int32),
            jax.ShapeDtypeStruct((SEQ, 128), jnp.int32),
            jax.ShapeDtypeStruct((SEQ, 128), jnp.int32),
            jax.ShapeDtypeStruct((SEQ + 8, 128), jnp.int32),
        ),
        in_specs=[vmem, vmem, vmem, any_space],
        out_specs=(any_space, any_space, vmem, vmem, vmem, vmem),
        scratch_shapes=[
            pltpu.VMEM((ROWS, WIDTH), jnp.bfloat16),
            pltpu.VMEM((4, 3, WIDTH, 256), jnp.bfloat16),
            pltpu.VMEM((HEADS, ROWS, 128), jnp.bfloat16),
            pltpu.VMEM((HEADS, ROWS // 2, 128), jnp.bfloat16),
            pltpu.VMEM((SEQ, 2, 128), jnp.int32),
            dma((4, 3)),
            dma((HEADS,)),
            dma((HEADS,)),
            dma((HEADS,)),
            dma((HEADS,)),
            dma((HEADS,)),
            dma((HEADS,)),
            dma((SEQ,)),
            dma((SEQ,)),
            dma((3,)),
        ],
        compiler_params=pltpu.CompilerParams(
            collective_id=1, has_side_effects=True, vmem_limit_bytes=VMEM_LIMIT
        ),
        name="spread",
    )(units, gain, meta, w_qkv)


def attend_kernel(range_ref, kv_ref, q_ref, seg_ref, out_ref, v1_ref, s_ref, qs_ref):
    core = lax.rem(lax.axis_index("seq"), 2)
    low = low_lanes(KEYS)

    def prepare(i, carry):
        at = pl.ds(pl.multiple_of(i * KEYS, KEYS), KEYS)
        v1_ref[at, :] = jnp.where(low, 1.0, kv_ref[at, :].astype(jnp.float32)).astype(
            jnp.bfloat16
        )
        return carry

    lax.fori_loop(0, UNITS // KEYS, prepare, 0)
    low_half = low_lanes(ROWS // 2)

    def pair(p, carry):
        rows = []
        for e in range(2):
            packed = q_ref[2 * p + e].astype(jnp.float32)
            rows.append(jnp.where(low_half, packed, 0.0))
            rows.append(jnp.where(low_half, pltpu.roll(packed, HEAD, 1), 0.0))
            seg_row = seg_ref[pl.ds(4 * p + 2 * e + core, 1), :].astype(jnp.float32)
            qs_ref[128 * e : 128 * e + 128, :] = jnp.transpose(
                jnp.broadcast_to(seg_row, (128, 128))
            )
        q = jnp.concatenate(rows, axis=0).astype(jnp.bfloat16)
        first = 4 * p + core
        lo, hi = range_ref[first, 0], range_ref[first + 2, 1]
        lo = lo // 128
        steps = (hi - 128 * lo + KEYS - 1) // KEYS
        base = jnp.minimum(lo, SEQ - (KEYS // 128) * steps)

        def score(i, top):
            block = base + (KEYS // 128) * i
            at = pl.ds(pl.multiple_of(block * 128, 128), KEYS)
            s = lax.dot_general(
                q, kv_ref[at, :], (((1,), (1,)), ((), ())), preferred_element_type=jnp.float32
            )
            for t in range(KEYS // 128):
                seg_row = seg_ref[pl.ds(block + t, 1), :].astype(jnp.float32)
                masked = jnp.where(qs_ref[...] == seg_row, s[:, 128 * t : 128 * t + 128], NEG)
                s_ref[i, :, 128 * t : 128 * t + 128] = masked
                top = jnp.maximum(top, masked)
            return top

        top = lax.fori_loop(0, steps, score, jnp.full((256, 128), NEG, jnp.float32))
        top = jnp.max(top, axis=1, keepdims=True)

        def gather(i, acc):
            at = pl.ds(pl.multiple_of((base + (KEYS // 128) * i) * 128, 128), KEYS)
            weights = jnp.exp(s_ref[i] - top).astype(jnp.bfloat16)
            return acc + jnp.dot(weights, v1_ref[at, :], preferred_element_type=jnp.float32)

        acc = lax.fori_loop(0, steps, gather, jnp.zeros((256, 128), jnp.float32))
        out = acc / pltpu.roll(acc, HEAD, 1)
        for e in range(2):
            upper, under = out[128 * e : 128 * e + 64], out[128 * e + 64 : 128 * e + 128]
            out_ref[2 * p + e] = jnp.where(low_half, pltpu.roll(upper, HEAD, 1), under).astype(
                jnp.bfloat16
            )
        return carry

    lax.fori_loop(0, CHIPS // 2, pair, 0)


def attend(ranges, kv, q, seg):
    vmem = pl.BlockSpec(memory_space=pltpu.VMEM)
    return pl.pallas_call(
        attend_kernel,
        out_shape=jax.ShapeDtypeStruct((CHIPS, ROWS // 2, 128), jnp.bfloat16),
        in_specs=[pl.BlockSpec(memory_space=pltpu.SMEM), vmem, vmem, vmem],
        out_specs=vmem,
        scratch_shapes=[
            pltpu.VMEM((UNITS, 128), jnp.bfloat16),
            pltpu.VMEM((UNITS // KEYS, 256, KEYS), jnp.float32),
            pltpu.VMEM((256, 128), jnp.float32),
        ],
        compiler_params=pltpu.CompilerParams(vmem_limit_bytes=VMEM_LIMIT),
        name="attend",
    )(ranges, kv.reshape(UNITS, 128), q, seg)


def mix_kernel(
    o_ref, units_ref, w_out_ref, w_proj_ref, out_ref, landed, attended, o_send, o_recv, own_sem
):
    me = lax.axis_index("seq")
    core = lax.rem(me, 2)
    chip = me // 2
    greet_all(me)
    await_all()

    def o_copy(target, source):
        return pltpu.make_async_remote_copy(
            src_ref=o_ref.at[target],
            dst_ref=landed.at[source],
            send_sem=o_send.at[target],
            recv_sem=o_recv.at[source],
            device_id=seq(2 * target + core),
            device_id_type=MESH,
        )

    def send(i, carry):
        o_copy(lax.rem(chip + i, CHIPS), chip).start()
        return carry

    lax.fori_loop(1, CHIPS, send, 0)
    own = pltpu.make_async_copy(o_ref.at[chip], landed.at[chip], own_sem)
    own.start()

    def receive(i, carry):
        source = lax.rem(chip + CHIPS - i, CHIPS)
        o_copy(source, source).wait()
        return carry

    lax.fori_loop(1, CHIPS, receive, 0)
    own.wait()

    low_half = low_lanes(ROWS // 2)
    for j in range(HEADS // 2):
        a, b = landed[2 * j].astype(jnp.float32), landed[2 * j + 1].astype(jnp.float32)
        upper = jnp.where(low_half, a, pltpu.roll(b, HEAD, 1))
        under = jnp.where(low_half, pltpu.roll(a, HEAD, 1), b)
        attended[:64, 128 * j : 128 * j + 128] = upper.astype(jnp.bfloat16)
        attended[64:, 128 * j : 128 * j + 128] = under.astype(jnp.bfloat16)
    mixed = jnp.dot(attended[...], w_out_ref[...], preferred_element_type=jnp.float32)
    mixed = (mixed + units_ref[...].astype(jnp.float32)).astype(jnp.bfloat16)
    out_ref[...] = jnp.dot(mixed, w_proj_ref[...], preferred_element_type=jnp.float32).astype(
        jnp.bfloat16
    )


def mix(o, units, w_out, w_proj):
    vmem = pl.BlockSpec(memory_space=pltpu.VMEM)
    dma = pltpu.SemaphoreType.DMA
    return pl.pallas_call(
        mix_kernel,
        out_shape=jax.ShapeDtypeStruct((ROWS, CHANNELS), jnp.bfloat16),
        in_specs=[vmem] * 4,
        out_specs=vmem,
        scratch_shapes=[
            pltpu.VMEM((HEADS, ROWS // 2, 128), jnp.bfloat16),
            pltpu.VMEM((ROWS, WIDTH), jnp.bfloat16),
            dma((CHIPS,)),
            dma((CHIPS,)),
            dma,
        ],
        compiler_params=pltpu.CompilerParams(
            collective_id=2, has_side_effects=True, vmem_limit_bytes=VMEM_LIMIT
        ),
        name="mix",
    )(o, units, w_out, w_proj)


def frames_kernel(
    range_ref, reduced_ref, start_ref, end_ref, w_ref, b_ref, gain_ref, out_ref, stacked
):
    me = lax.axis_index("seq")
    bias, gain = b_ref[...], gain_ref[...]

    def step(f, carry):
        block = jnp.minimum(range_ref[SEQ, f] // 128, SEQ - 2)
        starts = jnp.concatenate(
            [start_ref[pl.ds(block, 1), :], start_ref[pl.ds(block + 1, 1), :]], axis=1
        )
        ends = jnp.concatenate(
            [end_ref[pl.ds(block, 1), :], end_ref[pl.ds(block + 1, 1), :]], axis=1
        )
        window = reduced_ref[pl.ds(pl.multiple_of(block * 128, 128), 256), :]
        frame = (
            lax.broadcasted_iota(jnp.int32, (STEP, 256), 0)
            + FRAMES * me
            + STEP * f
            - KERNEL // 2
        )
        centre = None
        for j in range(KERNEL):
            chosen = jnp.where((frame + j >= starts) & (frame + j < ends), 1.0, 0.0)
            rows = jnp.dot(
                chosen.astype(jnp.bfloat16), window, preferred_element_type=jnp.float32
            )
            if j == KERNEL // 2:
                centre = rows
            stacked[:, CHANNELS * j : CHANNELS * j + CHANNELS] = rows.astype(jnp.bfloat16)
        conv = jnp.dot(stacked[...], w_ref[...], preferred_element_type=jnp.float32) + bias
        value = jnp.maximum(conv, 0.0)
        mean = jnp.mean(value, axis=-1, keepdims=True)
        centred = value - mean
        variance = jnp.mean(centred * centred, axis=-1, keepdims=True)
        result = centre + centred / jnp.sqrt(variance + 1e-05) * gain
        out_ref[pl.ds(pl.multiple_of(f * STEP, STEP), STEP), :] = result.astype(jnp.bfloat16)
        return carry

    lax.fori_loop(0, STEPS, step, 0)


def frames(ranges, reduced, starts, ends, conv_w, conv_b, conv_gain):
    vmem = pl.BlockSpec(memory_space=pltpu.VMEM)
    return pl.pallas_call(
        frames_kernel,
        out_shape=jax.ShapeDtypeStruct((FRAMES, CHANNELS), jnp.bfloat16),
        in_specs=[pl.BlockSpec(memory_space=pltpu.SMEM)] + [vmem] * 6,
        out_specs=vmem,
        scratch_shapes=[pltpu.VMEM((STEP, KERNEL * CHANNELS), jnp.bfloat16)],
        compiler_params=pltpu.CompilerParams(vmem_limit_bytes=VMEM_LIMIT),
        name="frames",
    )(ranges, reduced, starts, ends, conv_w, conv_b, conv_gain)


def local(units, durations, seg_ids, ln_gain, w_qkv, w_out, w_proj, conv_w, conv_b, conv_gain):
    meta = jnp.stack([seg_ids, durations])
    kv, q, seg, starts, ends, ranges = spread(units, ln_gain.reshape(1, WIDTH), meta, w_qkv)
    o = attend(ranges, kv, q, seg)
    reduced = mix(o, units, w_out, w_proj)
    whole = lax.all_gather(reduced, "seq", axis=0, tiled=True)
    return frames(
        ranges,
        whole,
        starts,
        ends,
        conv_w.reshape(KERNEL * CHANNELS, CHANNELS),
        conv_b.reshape(1, CHANNELS),
        conv_gain.reshape(1, CHANNELS),
    )


def solution(mesh):
    parted = P(("grp", "seq"))
    wide = P(("grp", "seq"), None)
    return jax.shard_map(
        local,
        mesh=mesh,
        in_specs=(wide, parted, parted) + (P(),) * 7,
        out_specs=wide,
        check_vma=False,
    )
```

```python
import functools

import jax
import jax.numpy as jnp
from jax import lax
from jax.experimental import pallas as pl
from jax.experimental.pallas import tpu as pltpu
from jax.sharding import PartitionSpec as P

MESH = pl.DeviceIdType.MESH
SEQ = 32
CHIPS = 16
HEADS = 16
HEAD = 64
ROWS = 128
WIDTH = 1024
UNITS = 4096
CHANNELS = 512
KERNEL = 5
FRAMES = 768
STEP = 96
STEPS = FRAMES // STEP
TILE = 256
BLOCKS = 8
GROUPS = 8
NEG = -1e30
MIB = 1024 * 1024
META = SEQ + 16


def seq(index):
    return {"seq": index}


def greet_all(me):
    barrier = pltpu.get_barrier_semaphore()

    def greet(i, carry):
        pl.semaphore_signal(
            barrier, 1, device_id=seq(lax.rem(me + i, SEQ)), device_id_type=MESH
        )
        return carry

    lax.fori_loop(1, SEQ, greet, 0)


def await_all(more=0):
    pl.semaphore_wait(pltpu.get_barrier_semaphore(), SEQ - 1 + more)


def group_at(own, i):
    flip = own + 1 - 2 * lax.rem(own, 2)
    if i == 0:
        return flip
    if i == 1:
        return lax.rem(flip + 2, 4)
    if i == 2:
        return lax.rem(own + 2, 4)
    return own


def low_lanes(rows):
    return lax.broadcasted_iota(jnp.int32, (rows, 128), 1) < HEAD


def spread_kernel(
    units_ref,
    gain_ref,
    meta_ref,
    w_ref,
    kv_ref,
    q_ref,
    mark_ref,
    seg_ref,
    start_ref,
    end_ref,
    range_ref,
    h_ref,
    wbuf,
    send_kv,
    send_q,
    meta_all,
    flags,
    w_sem,
    kv_send,
    kv_recv,
    q_send,
    q_recv,
    pass_send,
    pass_recv,
    meta_send,
    meta_recv,
    flag_send,
    flag_recv,
    own_sem,
):
    me = lax.axis_index("seq")
    part = lax.axis_index("grp")
    core = lax.rem(me, 2)
    chip = me // 2
    sibling = me + 1 - 2 * core
    own = chip // 4
    greet_all(me)

    def greet_part(i, carry):
        pl.semaphore_signal(
            pltpu.get_barrier_semaphore(),
            1,
            device_id={"grp": lax.rem(part + i, GROUPS)},
            device_id_type=MESH,
        )
        return carry

    lax.fori_loop(1, GROUPS, greet_part, 0)

    def w_copy(i, t):
        g = group_at(own, i)
        return pltpu.make_async_copy(
            w_ref.at[:, pl.ds(t * WIDTH + g * 256, 256)], wbuf.at[i, t], w_sem.at[i, t]
        )

    for i in range(4):
        for t in range(3):
            w_copy(i, t).start()

    x = units_ref[...].astype(jnp.float32)
    mean = jnp.mean(x, axis=-1, keepdims=True)
    centred = x - mean
    variance = jnp.mean(centred * centred, axis=-1, keepdims=True)
    h_ref[...] = (centred / jnp.sqrt(variance + 1e-05) * gain_ref[...]).astype(jnp.bfloat16)

    await_all(GROUPS - 1)

    def meta_copy(i, source):
        return pltpu.make_async_remote_copy(
            src_ref=meta_ref,
            dst_ref=meta_all.at[source],
            send_sem=meta_send.at[i],
            recv_sem=meta_recv.at[source],
            device_id=seq(lax.rem(me + i, SEQ)),
            device_id_type=MESH,
        )

    def send_meta(i, carry):
        meta_copy(i, me).start()
        return carry

    lax.fori_loop(1, SEQ, send_meta, 0)
    own_meta = pltpu.make_async_copy(meta_ref, meta_all.at[me], own_sem.at[2])
    own_meta.start()

    def kv_copy(head, source):
        return pltpu.make_async_remote_copy(
            src_ref=send_kv.at[head],
            dst_ref=kv_ref.at[2 * source + core],
            send_sem=kv_send.at[head],
            recv_sem=kv_recv.at[source],
            device_id=seq(2 * head + core),
            device_id_type=MESH,
        )

    def q_copy(head, source):
        return pltpu.make_async_remote_copy(
            src_ref=send_q.at[head],
            dst_ref=q_ref.at[source],
            send_sem=q_send.at[head],
            recv_sem=q_recv.at[source],
            device_id=seq(2 * head + core),
            device_id_type=MESH,
        )

    own_kv = pltpu.make_async_copy(send_kv.at[chip], kv_ref.at[me], own_sem.at[0])
    own_q = pltpu.make_async_copy(send_q.at[chip], q_ref.at[chip], own_sem.at[1])
    own_pass = pltpu.make_async_remote_copy(
        src_ref=send_kv.at[chip],
        dst_ref=kv_ref.at[me],
        send_sem=pass_send.at[chip],
        recv_sem=pass_recv.at[chip],
        device_id=seq(sibling),
        device_id_type=MESH,
    )

    low = low_lanes(ROWS // 2)
    for i in range(4):
        g = group_at(own, i)
        for t in range(3):
            w_copy(i, t).wait()
        h = h_ref[...]
        q4, k4, v4 = (
            jnp.dot(h, wbuf[i, t], preferred_element_type=jnp.float32) for t in range(3)
        )
        for j in range(2):
            at = slice(128 * j, 128 * j + 128)
            q2 = jnp.transpose(q4[:, at] * 0.125).astype(jnp.bfloat16)
            v2 = jnp.transpose(v4[:, at]).astype(jnp.bfloat16)
            k2 = k4[:, at]
            turned = pltpu.roll(k2, HEAD, 1)
            first = 4 * g + 2 * j
            send_kv[first, 0] = jnp.where(low, k2[:64], turned[64:]).astype(jnp.bfloat16)
            send_kv[first + 1, 0] = jnp.where(low, turned[:64], k2[64:]).astype(jnp.bfloat16)
            send_kv[first, 1] = v2[:64]
            send_kv[first + 1, 1] = v2[64:]
            send_q[first] = q2[:64]
            send_q[first + 1] = q2[64:]
        for r in range(4):
            head = 4 * g + lax.rem(chip + r, 4)
            if i < 3:
                kv_copy(head, chip).start()
                q_copy(head, chip).start()
            elif r == 0:
                own_kv.start()
                own_pass.start()
                own_q.start()
            else:
                kv_copy(head, chip).start()
                q_copy(head, chip).start()

    def await_meta(i, carry):
        meta_copy(i, lax.rem(me + SEQ - i, SEQ)).wait()
        return carry

    lax.fori_loop(1, SEQ, await_meta, 0)
    own_meta.wait()

    seg = meta_all[:, 0, :]
    dur = meta_all[:, 1, :].astype(jnp.float32)
    lower = (
        lax.broadcasted_iota(jnp.int32, (128, 128), 0)
        <= lax.broadcasted_iota(jnp.int32, (128, 128), 1)
    ).astype(jnp.float32).astype(jnp.bfloat16)
    earlier = (
        lax.broadcasted_iota(jnp.int32, (SEQ, SEQ), 0)
        > lax.broadcasted_iota(jnp.int32, (SEQ, SEQ), 1)
    ).astype(jnp.float32).astype(jnp.bfloat16)
    dur16 = dur.astype(jnp.bfloat16)
    within = jnp.dot(dur16, lower, preferred_element_type=jnp.float32)
    before = jnp.dot(earlier, dur16, preferred_element_type=jnp.float32)
    ends = within + jnp.sum(before, axis=1, keepdims=True)
    seg_ref[...] = seg
    start_ref[...] = (ends - dur).astype(jnp.int32)
    end_ref[...] = ends.astype(jnp.int32)

    first_frame = start_ref[:, 0:1]
    index = lax.broadcasted_iota(jnp.int32, (SEQ, 1), 0)
    late = (index >= 1) & (index <= SEQ - 3) & (first_frame > FRAMES * (index + 1) - 2)
    early = (index >= 3) & (first_frame < FRAMES * (index - 2) + FRAMES + 2)
    far = jnp.sum(jnp.where(late | early, 1.0, 0.0))
    flags[part] = jnp.zeros((8, 128), jnp.float32) + far

    def flag_copy(i, source):
        return pltpu.make_async_remote_copy(
            src_ref=flags.at[source],
            dst_ref=flags.at[source],
            send_sem=flag_send.at[i],
            recv_sem=flag_recv.at[source],
            device_id={"grp": lax.rem(part + i, GROUPS)},
            device_id_type=MESH,
        )

    def send_flag(i, carry):
        flag_copy(i, part).start()
        return carry

    lax.fori_loop(1, GROUPS, send_flag, 0)

    first_seg, last_seg = seg[:, 0:1], seg[:, 127:128]
    lane = lax.broadcasted_iota(jnp.int32, (SEQ, 128), 1)
    lo = jnp.zeros((SEQ, 1), jnp.int32)
    hi = jnp.zeros((SEQ, 1), jnp.int32)
    for s in range(8):
        below = jnp.sum((seg < s).astype(jnp.float32)).astype(jnp.int32)
        upto = jnp.sum((seg <= s).astype(jnp.float32)).astype(jnp.int32)
        lo = jnp.where(first_seg == s, below, lo)
        hi = jnp.where(last_seg == s, upto, hi)
    range_ref[0:SEQ, :] = jnp.where(lane == 0, lo, jnp.where(lane == 1, hi, 0))
    lane8 = lax.broadcasted_iota(jnp.int32, (8, 128), 1)
    block = jnp.zeros((8, 128), jnp.int32)
    for f in range(STEPS):
        t0 = (FRAMES * me + STEP * f - KERNEL // 2).astype(jnp.float32)
        passed = jnp.sum((ends <= t0).astype(jnp.float32)).astype(jnp.int32)
        block = jnp.where(lane8 == f, passed, block)
    range_ref[SEQ : SEQ + 8, :] = block

    def mark(b, carry):
        row = jnp.broadcast_to(meta_all[b, 0:1, :].astype(jnp.float32), (128, 128))
        column = jnp.transpose(row)
        place = lax.broadcasted_iota(jnp.int32, (64, 128), 1).astype(jnp.float32)
        marked = jnp.where(
            place < 8.0,
            jnp.where(place == column[:64], 1.0, 0.0),
            jnp.where(place == column[64:] + 8.0, 1.0, 0.0),
        )
        mark_ref[b] = marked.astype(jnp.bfloat16)
        return carry

    lax.fori_loop(0, SEQ, mark, 0)

    def await_flag(i, carry):
        flag_copy(i, lax.rem(part + GROUPS - i, GROUPS)).wait_recv()
        flag_copy(i, part).wait_send()
        return carry

    lax.fori_loop(1, GROUPS, await_flag, 0)
    total = flags[0]
    for i in range(1, GROUPS):
        total = total + flags[i]
    range_ref[SEQ + 8 :, :] = total.astype(jnp.int32)

    def passing(source):
        return pltpu.make_async_remote_copy(
            src_ref=kv_ref.at[2 * source + core],
            dst_ref=kv_ref.at[2 * source + core],
            send_sem=pass_send.at[source],
            recv_sem=pass_recv.at[source],
            device_id=seq(sibling),
            device_id_type=MESH,
        )

    for i in range(4):
        for r in range(4):
            if i == 3 and r == 0:
                continue
            source = 4 * group_at(own, i) + lax.rem(chip + 4 - r, 4)
            kv_copy(source, source).wait_recv()
            passing(source).start()

    for i in range(4):
        for r in range(4):
            source = 4 * group_at(own, i) + lax.rem(chip + 4 - r, 4)
            if i == 3 and r == 0:
                own_kv.wait()
                own_q.wait()
                own_pass.wait()
            else:
                q_copy(source, source).wait()
                kv_copy(source, source).wait_send()
                passing(source).wait()


def spread(units, gain, meta, w_qkv):
    any_space = pl.BlockSpec(memory_space=pl.ANY)
    vmem = pl.BlockSpec(memory_space=pltpu.VMEM)
    dma = pltpu.SemaphoreType.DMA
    return pl.pallas_call(
        spread_kernel,
        out_shape=(
            jax.ShapeDtypeStruct((SEQ, 2, ROWS // 2, 128), jnp.bfloat16),
            jax.ShapeDtypeStruct((CHIPS, HEAD, 128), jnp.bfloat16),
            jax.ShapeDtypeStruct((SEQ, ROWS // 2, 128), jnp.bfloat16),
            jax.ShapeDtypeStruct((SEQ, 128), jnp.int32),
            jax.ShapeDtypeStruct((SEQ, 128), jnp.int32),
            jax.ShapeDtypeStruct((SEQ, 128), jnp.int32),
            jax.ShapeDtypeStruct((META, 128), jnp.int32),
        ),
        in_specs=[vmem, vmem, vmem, any_space],
        out_specs=(any_space, any_space, vmem, vmem, vmem, vmem, vmem),
        scratch_shapes=[
            pltpu.VMEM((ROWS, WIDTH), jnp.bfloat16),
            pltpu.VMEM((4, 3, WIDTH, 256), jnp.bfloat16),
            pltpu.VMEM((HEADS, 2, ROWS // 2, 128), jnp.bfloat16),
            pltpu.VMEM((HEADS, HEAD, 128), jnp.bfloat16),
            pltpu.VMEM((SEQ, 2, 128), jnp.int32),
            pltpu.VMEM((GROUPS, 8, 128), jnp.float32),
            dma((4, 3)),
            dma((HEADS,)),
            dma((HEADS,)),
            dma((HEADS,)),
            dma((HEADS,)),
            dma((HEADS,)),
            dma((HEADS,)),
            dma((SEQ,)),
            dma((SEQ,)),
            dma((GROUPS,)),
            dma((GROUPS,)),
            dma((3,)),
        ],
        compiler_params=pltpu.CompilerParams(
            collective_id=1, has_side_effects=True, vmem_limit_bytes=16 * MIB
        ),
        name="spread",
    )(units, gain, meta, w_qkv)


def attend_kernel(range_ref, kv_ref, q_ref, mark_ref, seg_ref, out_ref, s_ref):
    core = lax.rem(lax.axis_index("seq"), 2)
    zero = jnp.zeros((64, 256), jnp.bfloat16)
    ones = jnp.ones((16, 128 * BLOCKS), jnp.bfloat16)

    def pair(p, carry):
        first = 4 * p + core
        lo, hi = range_ref[first, 0], range_ref[first + 2, 1]
        lo = lo // 128
        steps = (hi - 128 * lo + 128 * BLOCKS - 1) // (128 * BLOCKS)
        base = jnp.minimum(lo, SEQ - BLOCKS * steps)
        q = jnp.concatenate([q_ref[2 * p], q_ref[2 * p + 1]], axis=1)
        rows = lax.broadcasted_iota(jnp.int32, (8, 128), 0)
        bias = jnp.concatenate(
            [
                jnp.where(seg_ref[pl.ds(first + 2 * e, 1), :] == rows, 0.0, NEG)
                for e in range(2)
            ],
            axis=1,
        )
        none = jnp.zeros((8, 256), jnp.float32)
        biases = jnp.concatenate(
            [
                jnp.concatenate([bias, none], axis=0),
                jnp.concatenate([none, bias], axis=0),
            ],
            axis=1,
        ).astype(jnp.bfloat16)
        right = jnp.concatenate(
            [
                jnp.concatenate([q, zero], axis=1),
                jnp.concatenate([zero, q], axis=1),
                biases,
                jnp.zeros((112, 512), jnp.bfloat16),
            ],
            axis=0,
        )

        def score(i, top):
            block = base + BLOCKS * i
            left = jnp.concatenate(
                [
                    jnp.concatenate([kv_ref[block + t, 0], mark_ref[block + t]], axis=1)
                    for t in range(BLOCKS)
                ],
                axis=0,
            )
            s = jnp.dot(left, right, preferred_element_type=jnp.float32)
            s_ref[i] = s
            return jnp.maximum(top, jnp.max(s.reshape(8 * BLOCKS, 8, 512), axis=0))

        top = lax.fori_loop(0, steps, score, jnp.full((8, 512), NEG, jnp.float32))
        top = jnp.max(jnp.maximum(top[:, :256], top[:, 256:]), axis=0, keepdims=True)
        top = jnp.concatenate([top, top], axis=1)

        def gather(i, acc):
            block = base + BLOCKS * i
            w = jnp.exp(s_ref[i] - top).astype(jnp.bfloat16)
            wt = jnp.concatenate(
                [w[64 * t : 64 * t + 64, 256 * h : 256 * h + 256] for t in range(BLOCKS) for h in range(2)], axis=0
            )
            vt = jnp.concatenate([kv_ref[block + t, 1] for t in range(BLOCKS)], axis=1)
            vt = jnp.concatenate([vt, ones], axis=0)
            return acc + jnp.dot(vt, wt, preferred_element_type=jnp.float32)

        acc = lax.fori_loop(0, steps, gather, jnp.zeros((80, 256), jnp.float32))
        out = (acc[:64] / acc[64:65]).astype(jnp.bfloat16)
        out_ref[2 * p] = out[:, :128]
        out_ref[2 * p + 1] = out[:, 128:]
        return carry

    lax.fori_loop(0, CHIPS // 2, pair, 0)

def attend(ranges, kv, q, marks, seg):
    vmem = pl.BlockSpec(memory_space=pltpu.VMEM)
    return pl.pallas_call(
        attend_kernel,
        out_shape=jax.ShapeDtypeStruct((CHIPS, HEAD, 128), jnp.bfloat16),
        in_specs=[pl.BlockSpec(memory_space=pltpu.SMEM), vmem, vmem, vmem, vmem],
        out_specs=vmem,
        scratch_shapes=[pltpu.VMEM((SEQ // BLOCKS, 64 * BLOCKS, 512), jnp.float32)],
        compiler_params=pltpu.CompilerParams(vmem_limit_bytes=16 * MIB),
        name="attend",
    )(ranges, kv, q, marks, seg)


def send_back(o_ref, landed, o_send, o_recv, own_sem, me):
    core = lax.rem(me, 2)
    chip = me // 2

    def o_copy(target, source):
        return pltpu.make_async_remote_copy(
            src_ref=o_ref.at[target],
            dst_ref=landed.at[source],
            send_sem=o_send.at[target],
            recv_sem=o_recv.at[source],
            device_id=seq(2 * target + core),
            device_id_type=MESH,
        )

    def send(i, carry):
        o_copy(lax.rem(chip + i, CHIPS), chip).start()
        return carry

    lax.fori_loop(1, CHIPS, send, 0)
    own = pltpu.make_async_copy(o_ref.at[chip], landed.at[chip], own_sem)
    own.start()

    def receive(i, carry):
        source = lax.rem(chip + CHIPS - i, CHIPS)
        o_copy(source, source).wait()
        return carry

    lax.fori_loop(1, CHIPS, receive, 0)
    own.wait()


def project(landed, units_ref, w_out, w_proj):
    turned = [
        jnp.transpose(
            jnp.concatenate([landed[2 * j], landed[2 * j + 1]], axis=0).astype(jnp.float32)
        ).astype(jnp.bfloat16)
        for j in range(HEADS // 2)
    ]
    attended = jnp.concatenate(turned, axis=1)
    mixed = jnp.dot(attended, w_out, preferred_element_type=jnp.float32)
    mixed = (mixed + units_ref[...].astype(jnp.float32)).astype(jnp.bfloat16)
    return jnp.dot(mixed, w_proj, preferred_element_type=jnp.float32).astype(jnp.bfloat16)


def make_frames(
    me, base, last, range_ref, window_ref, start_ref, end_ref, w_ref, b_ref, gain_ref, out_ref, stacked
):
    for f in range(STEPS):
        block = jnp.clip(range_ref[SEQ, f] // 128, base, last)
        starts = jnp.concatenate(
            [start_ref[pl.ds(block, 1), :], start_ref[pl.ds(block + 1, 1), :]], axis=1
        )
        ends = jnp.concatenate(
            [end_ref[pl.ds(block, 1), :], end_ref[pl.ds(block + 1, 1), :]], axis=1
        )
        window = window_ref[pl.ds(block - base, 2)].reshape(256, CHANNELS)
        frame = lax.broadcasted_iota(jnp.int32, (STEP, 256), 0)
        first = FRAMES * me + STEP * f - KERNEL // 2
        starts, ends = starts - first, ends - first
        for j in range(KERNEL):
            chosen = jnp.where((frame >= starts - j) & (frame < ends - j), 1.0, 0.0)
            rows = jnp.dot(
                chosen.astype(jnp.bfloat16), window, preferred_element_type=jnp.float32
            )
            stacked[STEP * f : STEP * f + STEP, CHANNELS * j : CHANNELS * j + CHANNELS] = (
                rows.astype(jnp.bfloat16)
            )
    bias, gain = b_ref[...], gain_ref[...]
    for r in range(FRAMES // TILE):
        at = slice(TILE * r, TILE * r + TILE)
        conv = jnp.dot(stacked[at, :], w_ref[...], preferred_element_type=jnp.float32) + bias
        value = jnp.maximum(conv, 0.0)
        mean = jnp.mean(value, axis=-1, keepdims=True)
        centred = value - mean
        variance = jnp.mean(centred * centred, axis=-1, keepdims=True)
        half = KERNEL // 2
        centre = stacked[at, half * CHANNELS : (half + 1) * CHANNELS].astype(jnp.float32)
        result = centre + centred / jnp.sqrt(variance + 1e-05) * gain
        out_ref[at, :] = result.astype(jnp.bfloat16)


def finish_near_kernel(
    range_ref,
    o_ref,
    units_ref,
    w_out_ref,
    w_proj_ref,
    start_ref,
    end_ref,
    w_ref,
    b_ref,
    gain_ref,
    out_ref,
    landed,
    w_out,
    w_proj,
    conv_w,
    window,
    stacked,
    o_send,
    o_recv,
    near_send,
    near_recv,
    w_sem,
    own_sem,
):
    me = lax.axis_index("seq")
    greet_all(me)
    loads = [
        pltpu.make_async_copy(a, b, w_sem.at[i])
        for i, (a, b) in enumerate(((w_out_ref, w_out), (w_proj_ref, w_proj), (w_ref, conv_w)))
    ]
    for load in loads:
        load.start()
    await_all()
    send_back(o_ref, landed, o_send, o_recv, own_sem, me)
    loads[0].wait()
    loads[1].wait()

    def base_of(device):
        return jnp.clip(device - 1, 0, SEQ - 3)

    base = base_of(me)
    window[me - base] = project(landed, units_ref, w_out[...], w_proj[...])

    def near_copy(i, source, target):
        slot = source - base_of(target)
        return pltpu.make_async_remote_copy(
            src_ref=window.at[me - base],
            dst_ref=window.at[slot],
            send_sem=near_send.at[i],
            recv_sem=near_recv.at[slot],
            device_id=seq(target),
            device_id_type=MESH,
        )

    routes = (
        (me > 0, lax.rem(me + SEQ - 1, SEQ)),
        (me < SEQ - 1, lax.rem(me + 1, SEQ)),
        (me == 2, 0),
        (me == SEQ - 3, SEQ - 1),
    )
    for i, (present, target) in enumerate(routes):

        @pl.when(present)
        def _():
            near_copy(i, me, target).start()

    for slot in range(3):

        @pl.when(slot != me - base)
        def _():
            pltpu.make_async_remote_copy(
                src_ref=window.at[slot],
                dst_ref=window.at[slot],
                send_sem=near_send.at[0],
                recv_sem=near_recv.at[slot],
                device_id=seq(lax.rem(me + 1, SEQ)),
                device_id_type=MESH,
            ).wait_recv()

    loads[2].wait()
    make_frames(
        me, base, base + 1, range_ref, window, start_ref, end_ref, conv_w, b_ref, gain_ref, out_ref, stacked
    )
    for i, (present, target) in enumerate(routes):

        @pl.when(present)
        def _():
            near_copy(i, me, target).wait_send()


def finish_near(ranges, o, units, w_out, w_proj, starts, ends, conv_w, conv_b, conv_gain):
    vmem = pl.BlockSpec(memory_space=pltpu.VMEM)
    any_space = pl.BlockSpec(memory_space=pl.ANY)
    dma = pltpu.SemaphoreType.DMA
    return pl.pallas_call(
        finish_near_kernel,
        out_shape=jax.ShapeDtypeStruct((FRAMES, CHANNELS), jnp.bfloat16),
        in_specs=[pl.BlockSpec(memory_space=pltpu.SMEM), vmem, vmem, any_space, any_space]
        + [vmem, vmem, any_space, vmem, vmem],
        out_specs=vmem,
        scratch_shapes=[
            pltpu.VMEM((HEADS, HEAD, 128), jnp.bfloat16),
            pltpu.VMEM((WIDTH, WIDTH), jnp.bfloat16),
            pltpu.VMEM((WIDTH, CHANNELS), jnp.bfloat16),
            pltpu.VMEM((KERNEL * CHANNELS, CHANNELS), jnp.bfloat16),
            pltpu.VMEM((3, ROWS, CHANNELS), jnp.bfloat16),
            pltpu.VMEM((FRAMES, KERNEL * CHANNELS), jnp.bfloat16),
            dma((CHIPS,)),
            dma((CHIPS,)),
            dma((4,)),
            dma((3,)),
            dma((3,)),
            dma,
        ],
        compiler_params=pltpu.CompilerParams(
            collective_id=2, has_side_effects=True, vmem_limit_bytes=32 * MIB
        ),
        name="finish_near",
    )(ranges, o, units, w_out, w_proj, starts, ends, conv_w, conv_b, conv_gain)


def mix_kernel(
    o_ref, units_ref, w_out_ref, w_proj_ref, out_ref, landed, o_send, o_recv, own_sem
):
    me = lax.axis_index("seq")
    greet_all(me)
    await_all()
    send_back(o_ref, landed, o_send, o_recv, own_sem, me)
    out_ref[...] = project(landed, units_ref, w_out_ref[...], w_proj_ref[...])


def mix(o, units, w_out, w_proj):
    vmem = pl.BlockSpec(memory_space=pltpu.VMEM)
    dma = pltpu.SemaphoreType.DMA
    return pl.pallas_call(
        mix_kernel,
        out_shape=jax.ShapeDtypeStruct((ROWS, CHANNELS), jnp.bfloat16),
        in_specs=[vmem] * 4,
        out_specs=vmem,
        scratch_shapes=[
            pltpu.VMEM((HEADS, HEAD, 128), jnp.bfloat16),
            dma((CHIPS,)),
            dma((CHIPS,)),
            dma,
        ],
        compiler_params=pltpu.CompilerParams(
            collective_id=3, has_side_effects=True, vmem_limit_bytes=16 * MIB
        ),
        name="mix",
    )(o, units, w_out, w_proj)


def gather_kernel(block_ref, whole_ref, send_sem, recv_sem, own_sem):
    me = lax.axis_index("seq")
    greet_all(me)
    await_all()

    def copy(i, source):
        return pltpu.make_async_remote_copy(
            src_ref=block_ref,
            dst_ref=whole_ref.at[source],
            send_sem=send_sem.at[i],
            recv_sem=recv_sem.at[source],
            device_id=seq(lax.rem(me + i, SEQ)),
            device_id_type=MESH,
        )

    def send(i, carry):
        copy(i, me).start()
        return carry

    def receive(i, carry):
        copy(i, lax.rem(me + SEQ - i, SEQ)).wait()
        return carry

    lax.fori_loop(1, SEQ, send, 0)
    own = pltpu.make_async_copy(block_ref, whole_ref.at[me], own_sem)
    own.start()
    lax.fori_loop(1, SEQ, receive, 0)
    own.wait()


def gather(reduced):
    any_space = pl.BlockSpec(memory_space=pl.ANY)
    dma = pltpu.SemaphoreType.DMA
    return pl.pallas_call(
        gather_kernel,
        out_shape=jax.ShapeDtypeStruct((SEQ, ROWS, CHANNELS), jnp.bfloat16),
        in_specs=[any_space],
        out_specs=any_space,
        scratch_shapes=[dma((SEQ,)), dma((SEQ,)), dma],
        compiler_params=pltpu.CompilerParams(collective_id=4, has_side_effects=True),
        name="gather",
    )(reduced)


def frames_kernel(
    range_ref, whole_ref, start_ref, end_ref, w_ref, b_ref, gain_ref, out_ref, stacked
):
    make_frames(
        lax.axis_index("seq"),
        0,
        SEQ - 2,
        range_ref,
        whole_ref,
        start_ref,
        end_ref,
        w_ref,
        b_ref,
        gain_ref,
        out_ref,
        stacked,
    )


def frames(ranges, whole, starts, ends, conv_w, conv_b, conv_gain):
    vmem = pl.BlockSpec(memory_space=pltpu.VMEM)
    return pl.pallas_call(
        frames_kernel,
        out_shape=jax.ShapeDtypeStruct((FRAMES, CHANNELS), jnp.bfloat16),
        in_specs=[pl.BlockSpec(memory_space=pltpu.SMEM)] + [vmem] * 6,
        out_specs=vmem,
        scratch_shapes=[pltpu.VMEM((FRAMES, KERNEL * CHANNELS), jnp.bfloat16)],
        compiler_params=pltpu.CompilerParams(vmem_limit_bytes=32 * MIB),
        name="frames",
    )(ranges, whole, starts, ends, conv_w, conv_b, conv_gain)


def finish_far(ranges, o, units, w_out, w_proj, starts, ends, conv_w, conv_b, conv_gain):
    whole = gather(mix(o, units, w_out, w_proj))
    return frames(ranges, whole, starts, ends, conv_w, conv_b, conv_gain)


def local(units, durations, seg_ids, ln_gain, w_qkv, w_out, w_proj, conv_w, conv_b, conv_gain):
    meta = jnp.stack([seg_ids, durations])
    kv, q, marks, seg, starts, ends, ranges = spread(
        units, ln_gain.reshape(1, WIDTH), meta, w_qkv
    )
    o = attend(ranges, kv, q, marks, seg)
    return lax.cond(
        ranges[SEQ + 8, 0] == 0,
        finish_near,
        finish_far,
        ranges,
        o,
        units,
        w_out,
        w_proj,
        starts,
        ends,
        conv_w.reshape(KERNEL * CHANNELS, CHANNELS),
        conv_b.reshape(1, CHANNELS),
        conv_gain.reshape(1, CHANNELS),
    )


def solution(mesh):
    parted = P(("grp", "seq"))
    wide = P(("grp", "seq"), None)
    return jax.shard_map(
        local,
        mesh=mesh,
        in_specs=(wide, parted, parted) + (P(),) * 7,
        out_specs=wide,
        check_vma=False,
    )
```

```python
import functools

import jax
import jax.numpy as jnp
from jax import lax
from jax.experimental import pallas as pl
from jax.experimental.pallas import tpu as pltpu
from jax.sharding import PartitionSpec as P

MESH = pl.DeviceIdType.MESH
SEQ = 32
CHIPS = 16
HEADS = 16
HEAD = 64
ROWS = 128
WIDTH = 1024
UNITS = 4096
CHANNELS = 512
KERNEL = 5
FRAMES = 768
STEP = 96
STEPS = FRAMES // STEP
TILE = 256
BLOCKS = 8
GROUPS = 8
NEG = -1e30
MIB = 1024 * 1024
SPREAD_MIB = 56
META = SEQ + 16


def seq(index):
    return {"seq": index}


def greet(device):
    pl.semaphore_signal(
        pltpu.get_barrier_semaphore(), 1, device_id=device, device_id_type=MESH
    )


def greet_all(me):
    def one(i, carry):
        greet(seq(lax.rem(me + i, SEQ)))
        return carry

    lax.fori_loop(1, SEQ, one, 0)


def greet_row(me):
    def one(i, carry):
        greet(seq(lax.rem(me + 2 * i, SEQ)))
        return carry

    lax.fori_loop(1, CHIPS, one, 0)


def await_greetings(count):
    pl.semaphore_wait(pltpu.get_barrier_semaphore(), count)


def group_at(own, i):
    flip = own + 1 - 2 * lax.rem(own, 2)
    if i == 0:
        return flip
    if i == 1:
        return lax.rem(flip + 2, 4)
    if i == 2:
        return lax.rem(own + 2, 4)
    return own


def low_lanes(rows):
    return lax.broadcasted_iota(jnp.int32, (rows, 128), 1) < HEAD


def spread_kernel(
    units_ref,
    gain_ref,
    meta_ref,
    w_ref,
    kv_ref,
    q_ref,
    mark_ref,
    seg_ref,
    start_ref,
    end_ref,
    range_ref,
    h_ref,
    wbuf,
    send_kv,
    send_q,
    meta_all,
    flags,
    w_sem,
    kv_send,
    kv_recv,
    q_send,
    q_recv,
    pass_send,
    pass_recv,
    meta_send,
    meta_recv,
    flag_send,
    flag_recv,
    own_sem,
):
    me = lax.axis_index("seq")
    part = lax.axis_index("grp")
    core = lax.rem(me, 2)
    chip = me // 2
    sibling = me + 1 - 2 * core
    own = chip // 4
    greet_row(me)
    greet(seq(sibling))

    def greet_part(i, carry):
        greet({"grp": lax.rem(part + i, GROUPS)})
        return carry

    lax.fori_loop(1, GROUPS, greet_part, 0)

    def w_copy(i, t):
        g = group_at(own, i)
        return pltpu.make_async_copy(
            w_ref.at[:, pl.ds(t * WIDTH + g * 256, 256)], wbuf.at[i, t], w_sem.at[i, t]
        )

    for i in range(4):
        w_copy(i, 1).start()
        w_copy(i, 2).start()
    for i in range(4):
        w_copy(i, 0).start()

    x = units_ref[...].astype(jnp.float32)
    mean = jnp.mean(x, axis=-1, keepdims=True)
    centred = x - mean
    variance = jnp.mean(centred * centred, axis=-1, keepdims=True)
    h_ref[...] = (centred / jnp.sqrt(variance + 1e-05) * gain_ref[...]).astype(jnp.bfloat16)

    def meta_copy(i, source):
        return pltpu.make_async_remote_copy(
            src_ref=meta_ref,
            dst_ref=meta_all.at[source, core],
            send_sem=meta_send.at[i],
            recv_sem=meta_recv.at[source],
            device_id=seq(lax.rem(me + 2 * i, SEQ)),
            device_id_type=MESH,
        )

    def send_meta(i, carry):
        meta_copy(i, chip).start()
        return carry

    own_meta = pltpu.make_async_copy(meta_ref, meta_all.at[chip, core], own_sem.at[2])
    pass_meta = pltpu.make_async_remote_copy(
        src_ref=meta_all.at[:, core],
        dst_ref=meta_all.at[:, core],
        send_sem=meta_send.at[0],
        recv_sem=own_sem.at[3],
        device_id=seq(sibling),
        device_id_type=MESH,
    )

    def kv_copy(head, source):
        return pltpu.make_async_remote_copy(
            src_ref=send_kv.at[head],
            dst_ref=kv_ref.at[2 * source + core],
            send_sem=kv_send.at[head],
            recv_sem=kv_recv.at[source],
            device_id=seq(2 * head + core),
            device_id_type=MESH,
        )

    def q_copy(head, source):
        return pltpu.make_async_remote_copy(
            src_ref=send_q.at[head],
            dst_ref=q_ref.at[source],
            send_sem=q_send.at[head],
            recv_sem=q_recv.at[source],
            device_id=seq(2 * head + core),
            device_id_type=MESH,
        )

    own_kv = pltpu.make_async_copy(send_kv.at[chip], kv_ref.at[me], own_sem.at[0])
    own_q = pltpu.make_async_copy(send_q.at[chip], q_ref.at[chip], own_sem.at[1])
    own_pass = pltpu.make_async_remote_copy(
        src_ref=send_kv.at[chip],
        dst_ref=kv_ref.at[me],
        send_sem=pass_send.at[chip],
        recv_sem=pass_recv.at[chip],
        device_id=seq(sibling),
        device_id_type=MESH,
    )

    low = low_lanes(ROWS // 2)
    for i in range(4):
        g = group_at(own, i)
        w_copy(i, 1).wait()
        w_copy(i, 2).wait()
        h = h_ref[...]
        k4, v4 = (
            jnp.dot(h, wbuf[i, t], preferred_element_type=jnp.float32) for t in (1, 2)
        )
        for j in range(2):
            at = slice(128 * j, 128 * j + 128)
            v2 = jnp.transpose(v4[:, at]).astype(jnp.bfloat16)
            k2 = k4[:, at]
            turned = pltpu.roll(k2, HEAD, 1)
            first = 4 * g + 2 * j
            send_kv[first, 0] = jnp.where(low, k2[:64], turned[64:]).astype(jnp.bfloat16)
            send_kv[first + 1, 0] = jnp.where(low, turned[:64], k2[64:]).astype(jnp.bfloat16)
            send_kv[first, 1] = v2[:64]
            send_kv[first + 1, 1] = v2[64:]
        if i == 0:
            await_greetings(CHIPS - 1 + 1 + GROUPS - 1)
        for r in range(4):
            if i == 3 and r == 0:
                own_kv.start()
                own_pass.start()
            else:
                kv_copy(4 * g + lax.rem(chip + r, 4), chip).start()
        if i == 0:
            lax.fori_loop(1, CHIPS, send_meta, 0)
            own_meta.start()
    for i in range(4):
        g = group_at(own, i)
        w_copy(i, 0).wait()
        q4 = jnp.dot(h_ref[...], wbuf[i, 0], preferred_element_type=jnp.float32) * 0.125
        for j in range(2):
            q2 = jnp.transpose(q4[:, 128 * j : 128 * j + 128]).astype(jnp.bfloat16)
            first = 4 * g + 2 * j
            send_q[first] = q2[:64]
            send_q[first + 1] = q2[64:]
        for r in range(4):
            if i == 3 and r == 0:
                own_q.start()
            else:
                q_copy(4 * g + lax.rem(chip + r, 4), chip).start()

    def await_meta(i, carry):
        meta_copy(i, lax.rem(chip + CHIPS - i, CHIPS)).wait()
        return carry

    lax.fori_loop(1, CHIPS, await_meta, 0)
    own_meta.wait()
    pass_meta.start()
    pass_meta.wait()
    meta = meta_all[...].reshape(SEQ, 2, 128)

    seg = meta[:, 0, :]
    dur = meta[:, 1, :].astype(jnp.float32)
    lower = (
        lax.broadcasted_iota(jnp.int32, (128, 128), 0)
        <= lax.broadcasted_iota(jnp.int32, (128, 128), 1)
    ).astype(jnp.float32).astype(jnp.bfloat16)
    earlier = (
        lax.broadcasted_iota(jnp.int32, (SEQ, SEQ), 0)
        > lax.broadcasted_iota(jnp.int32, (SEQ, SEQ), 1)
    ).astype(jnp.float32).astype(jnp.bfloat16)
    dur16 = dur.astype(jnp.bfloat16)
    within = jnp.dot(dur16, lower, preferred_element_type=jnp.float32)
    before = jnp.dot(earlier, dur16, preferred_element_type=jnp.float32)
    ends = within + jnp.sum(before, axis=1, keepdims=True)
    seg_ref[...] = seg
    start_ref[...] = (ends - dur).astype(jnp.int32)
    end_ref[...] = ends.astype(jnp.int32)

    first_frame = start_ref[:, 0:1]
    index = lax.broadcasted_iota(jnp.int32, (SEQ, 1), 0)
    late = (index >= 1) & (index <= SEQ - 3) & (first_frame > FRAMES * (index + 1) - 2)
    early = (index >= 3) & (first_frame < FRAMES * (index - 2) + FRAMES + 2)
    far = jnp.sum(jnp.where(late | early, 1.0, 0.0))
    flags[part] = jnp.zeros((8, 128), jnp.float32) + far

    def flag_copy(i, source):
        return pltpu.make_async_remote_copy(
            src_ref=flags.at[source],
            dst_ref=flags.at[source],
            send_sem=flag_send.at[i],
            recv_sem=flag_recv.at[source],
            device_id={"grp": lax.rem(part + i, GROUPS)},
            device_id_type=MESH,
        )

    def send_flag(i, carry):
        flag_copy(i, part).start()
        return carry

    lax.fori_loop(1, GROUPS, send_flag, 0)

    first_seg, last_seg = seg[:, 0:1], seg[:, 127:128]
    lane = lax.broadcasted_iota(jnp.int32, (SEQ, 128), 1)
    lo = jnp.zeros((SEQ, 1), jnp.int32)
    hi = jnp.zeros((SEQ, 1), jnp.int32)
    for s in range(8):
        below = jnp.sum((seg < s).astype(jnp.float32)).astype(jnp.int32)
        upto = jnp.sum((seg <= s).astype(jnp.float32)).astype(jnp.int32)
        lo = jnp.where(first_seg == s, below, lo)
        hi = jnp.where(last_seg == s, upto, hi)
    range_ref[0:SEQ, :] = jnp.where(lane == 0, lo, jnp.where(lane == 1, hi, 0))
    lane8 = lax.broadcasted_iota(jnp.int32, (8, 128), 1)
    block = jnp.zeros((8, 128), jnp.int32)
    for f in range(STEPS):
        t0 = (FRAMES * me + STEP * f - KERNEL // 2).astype(jnp.float32)
        passed = jnp.sum((ends <= t0).astype(jnp.float32)).astype(jnp.int32)
        block = jnp.where(lane8 == f, passed, block)
    range_ref[SEQ : SEQ + 8, :] = block

    def mark(b, carry):
        row = jnp.broadcast_to(seg_ref[pl.ds(b, 1), :].astype(jnp.float32), (128, 128))
        column = jnp.transpose(row)
        place = lax.broadcasted_iota(jnp.int32, (64, 128), 1).astype(jnp.float32)
        marked = jnp.where(
            place < 8.0,
            jnp.where(place == column[:64], 1.0, 0.0),
            jnp.where(place == column[64:] + 8.0, 1.0, 0.0),
        )
        mark_ref[b] = marked.astype(jnp.bfloat16)
        return carry

    lax.fori_loop(0, SEQ, mark, 0)

    def await_flag(i, carry):
        flag_copy(i, lax.rem(part + GROUPS - i, GROUPS)).wait_recv()
        flag_copy(i, part).wait_send()
        return carry

    lax.fori_loop(1, GROUPS, await_flag, 0)
    total = flags[0]
    for i in range(1, GROUPS):
        total = total + flags[i]
    range_ref[SEQ + 8 :, :] = total.astype(jnp.int32)

    def passing(source):
        return pltpu.make_async_remote_copy(
            src_ref=kv_ref.at[2 * source + core],
            dst_ref=kv_ref.at[2 * source + core],
            send_sem=pass_send.at[source],
            recv_sem=pass_recv.at[source],
            device_id=seq(sibling),
            device_id_type=MESH,
        )

    for i in range(4):
        for r in range(4):
            if i == 3 and r == 0:
                continue
            source = 4 * group_at(own, i) + lax.rem(chip + 4 - r, 4)
            kv_copy(source, source).wait_recv()
            passing(source).start()

    for i in range(4):
        for r in range(4):
            source = 4 * group_at(own, i) + lax.rem(chip + 4 - r, 4)
            if i == 3 and r == 0:
                own_kv.wait()
                own_q.wait()
                own_pass.wait()
            else:
                q_copy(source, source).wait()
                kv_copy(source, source).wait_send()
                passing(source).wait()


def spread(units, gain, meta, w_qkv):
    any_space = pl.BlockSpec(memory_space=pl.ANY)
    vmem = pl.BlockSpec(memory_space=pltpu.VMEM)
    dma = pltpu.SemaphoreType.DMA
    return pl.pallas_call(
        spread_kernel,
        out_shape=(
            jax.ShapeDtypeStruct((SEQ, 2, ROWS // 2, 128), jnp.bfloat16),
            jax.ShapeDtypeStruct((CHIPS, HEAD, 128), jnp.bfloat16),
            jax.ShapeDtypeStruct((SEQ, ROWS // 2, 128), jnp.bfloat16),
            jax.ShapeDtypeStruct((SEQ, 128), jnp.int32),
            jax.ShapeDtypeStruct((SEQ, 128), jnp.int32),
            jax.ShapeDtypeStruct((SEQ, 128), jnp.int32),
            jax.ShapeDtypeStruct((META, 128), jnp.int32),
        ),
        in_specs=[vmem, vmem, vmem, any_space],
        out_specs=(any_space, any_space, vmem, vmem, vmem, vmem, vmem),
        scratch_shapes=[
            pltpu.VMEM((ROWS, WIDTH), jnp.bfloat16),
            pltpu.VMEM((4, 3, WIDTH, 256), jnp.bfloat16),
            pltpu.VMEM((HEADS, 2, ROWS // 2, 128), jnp.bfloat16),
            pltpu.VMEM((HEADS, HEAD, 128), jnp.bfloat16),
            pltpu.VMEM((CHIPS, 2, 2, 128), jnp.int32),
            pltpu.VMEM((GROUPS, 8, 128), jnp.float32),
            dma((4, 3)),
            dma((HEADS,)),
            dma((HEADS,)),
            dma((HEADS,)),
            dma((HEADS,)),
            dma((HEADS,)),
            dma((HEADS,)),
            dma((CHIPS,)),
            dma((CHIPS,)),
            dma((GROUPS,)),
            dma((GROUPS,)),
            dma((4,)),
        ],
        compiler_params=pltpu.CompilerParams(
            collective_id=1, has_side_effects=True, vmem_limit_bytes=SPREAD_MIB * MIB
        ),
        name="spread",
    )(units, gain, meta, w_qkv)


def attend_kernel(range_ref, kv_ref, q_ref, mark_ref, seg_ref, out_ref, even_ref, odd_ref):
    core = lax.rem(lax.axis_index("seq"), 2)
    pairs = CHIPS // 2
    ones = jnp.ones((16, 128 * BLOCKS), jnp.bfloat16)

    def extent(p):
        first = 4 * p + core
        lo, hi = range_ref[first, 0] // 128, range_ref[first + 2, 1]
        steps = (hi - 128 * lo + 128 * BLOCKS - 1) // (128 * BLOCKS)
        return jnp.minimum(lo, SEQ - BLOCKS * steps), steps

    def right_side(p):
        first = 4 * p + core
        q = jnp.concatenate([q_ref[2 * p], q_ref[2 * p + 1]], axis=1)
        zero = jnp.zeros((HEAD, 256), jnp.bfloat16)
        rows = lax.broadcasted_iota(jnp.int32, (8, 128), 0)
        bias = jnp.concatenate(
            [
                jnp.where(seg_ref[pl.ds(first + 2 * e, 1), :] == rows, 0.0, NEG)
                for e in range(2)
            ],
            axis=1,
        )
        none = jnp.zeros((8, 256), jnp.float32)
        biases = jnp.concatenate(
            [jnp.concatenate([bias, none], axis=0), jnp.concatenate([none, bias], axis=0)],
            axis=1,
        ).astype(jnp.bfloat16)
        return jnp.concatenate(
            [
                jnp.concatenate([q, zero], axis=1),
                jnp.concatenate([zero, q], axis=1),
                biases,
                jnp.zeros((112, 512), jnp.bfloat16),
            ],
            axis=0,
        )

    def score(right, block, keep, top):
        left = jnp.concatenate(
            [
                jnp.concatenate([kv_ref[block + t, 0], mark_ref[block + t]], axis=1)
                for t in range(BLOCKS)
            ],
            axis=0,
        )
        s = jnp.dot(left, right, preferred_element_type=jnp.float32)
        keep[...] = s
        return jnp.maximum(top, jnp.max(s.reshape(8 * BLOCKS, 8, 512), axis=0))

    def collect(top, block, kept, acc):
        w = jnp.exp(kept[...] - top).astype(jnp.bfloat16)
        w = jnp.concatenate(
            [
                w[64 * t : 64 * t + 64, 256 * h : 256 * h + 256]
                for t in range(BLOCKS)
                for h in range(2)
            ],
            axis=0,
        )
        v = jnp.concatenate([kv_ref[block + t, 1] for t in range(BLOCKS)], axis=1)
        v = jnp.concatenate([v, ones], axis=0)
        return acc + jnp.dot(v, w, preferred_element_type=jnp.float32)

    def peak(top):
        top = jnp.max(jnp.maximum(top[:, :256], top[:, 256:]), axis=0, keepdims=True)
        return jnp.concatenate([top, top], axis=1)

    def give(p, acc):
        out = (acc[:HEAD] / acc[HEAD : HEAD + 1]).astype(jnp.bfloat16)
        out_ref[2 * p] = out[:, :128]
        out_ref[2 * p + 1] = out[:, 128:]

    low = jnp.full((8, 512), NEG, jnp.float32)
    clear = jnp.zeros((HEAD + 16, 256), jnp.float32)
    base0, steps0 = extent(0)
    right0 = right_side(0)
    top0 = lax.fori_loop(
        0, steps0, lambda i, top: score(right0, base0 + BLOCKS * i, even_ref.at[i], top), low
    )

    def both(p, here, there, top):
        base, steps = extent(p)
        old_base, old_steps = extent(p - 1)
        right = right_side(p)

        def run(count):
            new_top, acc = low, clear
            for i in range(count):
                j = jnp.minimum(i, steps - 1)
                new_top = score(right, base + BLOCKS * j, here.at[j], new_top)
                k = jnp.minimum(i, old_steps - 1)
                level = jnp.where(i < old_steps, top, -NEG)
                acc = collect(level, old_base + BLOCKS * k, there.at[k], acc)
            return new_top, acc

        new_top, acc = lax.switch(
            jnp.maximum(steps, old_steps) - 1,
            [functools.partial(run, count + 1) for count in range(SEQ // BLOCKS)],
        )
        give(p - 1, acc)
        return peak(new_top)

    def two(i, top):
        top = both(2 * i + 1, odd_ref, even_ref, top)
        return both(2 * i + 2, even_ref, odd_ref, top)

    top = lax.fori_loop(0, pairs // 2 - 1, two, peak(top0))
    top = both(pairs - 1, odd_ref, even_ref, top)
    last = pairs - 1
    base, steps = extent(last)
    acc = lax.fori_loop(
        0,
        steps,
        lambda i, acc: collect(top, base + BLOCKS * i, odd_ref.at[i], acc),
        clear,
    )
    give(last, acc)


def attend(ranges, kv, q, marks, seg):
    vmem = pl.BlockSpec(memory_space=pltpu.VMEM)
    return pl.pallas_call(
        attend_kernel,
        out_shape=jax.ShapeDtypeStruct((CHIPS, HEAD, 128), jnp.bfloat16),
        in_specs=[pl.BlockSpec(memory_space=pltpu.SMEM), vmem, vmem, vmem, vmem],
        out_specs=vmem,
        scratch_shapes=[pltpu.VMEM((SEQ // BLOCKS, 64 * BLOCKS, 512), jnp.float32)] * 2,
        compiler_params=pltpu.CompilerParams(vmem_limit_bytes=24 * MIB),
        name="attend",
    )(ranges, kv, q, marks, seg)


def send_back(o_ref, landed, o_send, o_recv, own_sem, me):
    core = lax.rem(me, 2)
    chip = me // 2

    def o_copy(target, source):
        return pltpu.make_async_remote_copy(
            src_ref=o_ref.at[target],
            dst_ref=landed.at[source],
            send_sem=o_send.at[target],
            recv_sem=o_recv.at[source],
            device_id=seq(2 * target + core),
            device_id_type=MESH,
        )

    def send(i, carry):
        o_copy(lax.rem(chip + i, CHIPS), chip).start()
        return carry

    lax.fori_loop(1, CHIPS, send, 0)
    own = pltpu.make_async_copy(o_ref.at[chip], landed.at[chip], own_sem)
    own.start()

    def receive(i, carry):
        source = lax.rem(chip + CHIPS - i, CHIPS)
        o_copy(source, source).wait()
        return carry

    lax.fori_loop(1, CHIPS, receive, 0)
    own.wait()


def project(landed, units_ref, w_out, w_proj):
    turned = [
        jnp.transpose(
            jnp.concatenate([landed[2 * j], landed[2 * j + 1]], axis=0).astype(jnp.float32)
        ).astype(jnp.bfloat16)
        for j in range(HEADS // 2)
    ]
    attended = jnp.concatenate(turned, axis=1)
    mixed = jnp.dot(attended, w_out, preferred_element_type=jnp.float32)
    mixed = (mixed + units_ref[...].astype(jnp.float32)).astype(jnp.bfloat16)
    return jnp.dot(mixed, w_proj, preferred_element_type=jnp.float32).astype(jnp.bfloat16)


def make_frames(
    me, base, last, range_ref, window_ref, start_ref, end_ref, w_ref, b_ref, gain_ref, out_ref, stacked
):
    for f in range(STEPS):
        block = jnp.clip(range_ref[SEQ, f] // 128, base, last)
        starts = jnp.concatenate(
            [start_ref[pl.ds(block, 1), :], start_ref[pl.ds(block + 1, 1), :]], axis=1
        )
        ends = jnp.concatenate(
            [end_ref[pl.ds(block, 1), :], end_ref[pl.ds(block + 1, 1), :]], axis=1
        )
        window = window_ref[pl.ds(block - base, 2)].reshape(256, CHANNELS)
        frame = lax.broadcasted_iota(jnp.int32, (STEP, 256), 0)
        first = FRAMES * me + STEP * f - KERNEL // 2
        starts, ends = starts - first, ends - first
        for j in range(KERNEL):
            chosen = jnp.where((frame >= starts - j) & (frame < ends - j), 1.0, 0.0)
            rows = jnp.dot(
                chosen.astype(jnp.bfloat16), window, preferred_element_type=jnp.float32
            )
            stacked[STEP * f : STEP * f + STEP, CHANNELS * j : CHANNELS * j + CHANNELS] = (
                rows.astype(jnp.bfloat16)
            )
    bias, gain = b_ref[...], gain_ref[...]
    for r in range(FRAMES // TILE):
        at = slice(TILE * r, TILE * r + TILE)
        conv = jnp.dot(stacked[at, :], w_ref[...], preferred_element_type=jnp.float32) + bias
        value = jnp.maximum(conv, 0.0)
        mean = jnp.mean(value, axis=-1, keepdims=True)
        centred = value - mean
        variance = jnp.mean(centred * centred, axis=-1, keepdims=True)
        half = KERNEL // 2
        centre = stacked[at, half * CHANNELS : (half + 1) * CHANNELS].astype(jnp.float32)
        result = centre + centred / jnp.sqrt(variance + 1e-05) * gain
        out_ref[at, :] = result.astype(jnp.bfloat16)


def finish_near_kernel(
    range_ref,
    o_ref,
    units_ref,
    w_out_ref,
    w_proj_ref,
    start_ref,
    end_ref,
    w_ref,
    b_ref,
    gain_ref,
    out_ref,
    landed,
    units,
    w_out,
    w_proj,
    conv_w,
    window,
    stacked,
    o_send,
    o_recv,
    near_send,
    near_recv,
    w_sem,
    own_sem,
):
    me = lax.axis_index("seq")
    greet_row(me)
    for there in (-1, 1):

        @pl.when((me + there >= 0) & (me + there < SEQ))
        def _():
            greet(seq(lax.rem(me + SEQ + there, SEQ)))

    loads = [
        pltpu.make_async_copy(a, b, w_sem.at[i])
        for i, (a, b) in enumerate(
            (
                (units_ref, units),
                (w_out_ref, w_out),
                (w_proj_ref, w_proj),
                (w_ref, conv_w),
            )
        )
    ]
    for load in loads:
        load.start()
    await_greetings(
        CHIPS - 1 + jnp.where(me > 0, 1, 0) + jnp.where(me < SEQ - 1, 1, 0)
    )
    send_back(o_ref, landed, o_send, o_recv, own_sem, me)
    for load in loads[:3]:
        load.wait()

    def base_of(device):
        return jnp.clip(device - 1, 0, SEQ - 3)

    base = base_of(me)
    window[me - base] = project(landed, units, w_out[...], w_proj[...])

    def near_copy(i, source, target):
        slot = source - base_of(target)
        return pltpu.make_async_remote_copy(
            src_ref=window.at[me - base],
            dst_ref=window.at[slot],
            send_sem=near_send.at[i],
            recv_sem=near_recv.at[slot],
            device_id=seq(target),
            device_id_type=MESH,
        )

    routes = (
        (me > 0, lax.rem(me + SEQ - 1, SEQ)),
        (me < SEQ - 1, lax.rem(me + 1, SEQ)),
        (me == 2, 0),
        (me == SEQ - 3, SEQ - 1),
    )
    for i, (present, target) in enumerate(routes):

        @pl.when(present)
        def _():
            near_copy(i, me, target).start()

    for slot in range(3):

        @pl.when(slot != me - base)
        def _():
            pltpu.make_async_remote_copy(
                src_ref=window.at[slot],
                dst_ref=window.at[slot],
                send_sem=near_send.at[0],
                recv_sem=near_recv.at[slot],
                device_id=seq(lax.rem(me + 1, SEQ)),
                device_id_type=MESH,
            ).wait_recv()

    loads[3].wait()
    make_frames(
        me, base, base + 1, range_ref, window, start_ref, end_ref, conv_w, b_ref, gain_ref, out_ref, stacked
    )
    for i, (present, target) in enumerate(routes):

        @pl.when(present)
        def _():
            near_copy(i, me, target).wait_send()


def finish_near(ranges, o, units, w_out, w_proj, starts, ends, conv_w, conv_b, conv_gain):
    vmem = pl.BlockSpec(memory_space=pltpu.VMEM)
    any_space = pl.BlockSpec(memory_space=pl.ANY)
    dma = pltpu.SemaphoreType.DMA
    return pl.pallas_call(
        finish_near_kernel,
        out_shape=jax.ShapeDtypeStruct((FRAMES, CHANNELS), jnp.bfloat16),
        in_specs=[pl.BlockSpec(memory_space=pltpu.SMEM), any_space, any_space, any_space, any_space]
        + [vmem, vmem, any_space, vmem, vmem],
        out_specs=vmem,
        scratch_shapes=[
            pltpu.VMEM((HEADS, HEAD, 128), jnp.bfloat16),
            pltpu.VMEM((ROWS, WIDTH), jnp.bfloat16),
            pltpu.VMEM((WIDTH, WIDTH), jnp.bfloat16),
            pltpu.VMEM((WIDTH, CHANNELS), jnp.bfloat16),
            pltpu.VMEM((KERNEL * CHANNELS, CHANNELS), jnp.bfloat16),
            pltpu.VMEM((3, ROWS, CHANNELS), jnp.bfloat16),
            pltpu.VMEM((FRAMES, KERNEL * CHANNELS), jnp.bfloat16),
            dma((CHIPS,)),
            dma((CHIPS,)),
            dma((4,)),
            dma((3,)),
            dma((4,)),
            dma,
        ],
        compiler_params=pltpu.CompilerParams(
            collective_id=2, has_side_effects=True, vmem_limit_bytes=32 * MIB
        ),
        name="finish_near",
    )(ranges, o, units, w_out, w_proj, starts, ends, conv_w, conv_b, conv_gain)


def mix_kernel(
    o_ref, units_ref, w_out_ref, w_proj_ref, out_ref, landed, o_send, o_recv, own_sem
):
    me = lax.axis_index("seq")
    greet_all(me)
    await_greetings(SEQ - 1)
    send_back(o_ref, landed, o_send, o_recv, own_sem, me)
    out_ref[...] = project(landed, units_ref, w_out_ref[...], w_proj_ref[...])


def mix(o, units, w_out, w_proj):
    vmem = pl.BlockSpec(memory_space=pltpu.VMEM)
    dma = pltpu.SemaphoreType.DMA
    return pl.pallas_call(
        mix_kernel,
        out_shape=jax.ShapeDtypeStruct((ROWS, CHANNELS), jnp.bfloat16),
        in_specs=[vmem] * 4,
        out_specs=vmem,
        scratch_shapes=[
            pltpu.VMEM((HEADS, HEAD, 128), jnp.bfloat16),
            dma((CHIPS,)),
            dma((CHIPS,)),
            dma,
        ],
        compiler_params=pltpu.CompilerParams(
            collective_id=3, has_side_effects=True, vmem_limit_bytes=16 * MIB
        ),
        name="mix",
    )(o, units, w_out, w_proj)


def gather_kernel(block_ref, whole_ref, send_sem, recv_sem, own_sem):
    me = lax.axis_index("seq")
    greet_all(me)
    await_greetings(SEQ - 1)

    def copy(i, source):
        return pltpu.make_async_remote_copy(
            src_ref=block_ref,
            dst_ref=whole_ref.at[source],
            send_sem=send_sem.at[i],
            recv_sem=recv_sem.at[source],
            device_id=seq(lax.rem(me + i, SEQ)),
            device_id_type=MESH,
        )

    def send(i, carry):
        copy(i, me).start()
        return carry

    def receive(i, carry):
        copy(i, lax.rem(me + SEQ - i, SEQ)).wait()
        return carry

    lax.fori_loop(1, SEQ, send, 0)
    own = pltpu.make_async_copy(block_ref, whole_ref.at[me], own_sem)
    own.start()
    lax.fori_loop(1, SEQ, receive, 0)
    own.wait()


def gather(reduced):
    any_space = pl.BlockSpec(memory_space=pl.ANY)
    dma = pltpu.SemaphoreType.DMA
    return pl.pallas_call(
        gather_kernel,
        out_shape=jax.ShapeDtypeStruct((SEQ, ROWS, CHANNELS), jnp.bfloat16),
        in_specs=[any_space],
        out_specs=any_space,
        scratch_shapes=[dma((SEQ,)), dma((SEQ,)), dma],
        compiler_params=pltpu.CompilerParams(collective_id=4, has_side_effects=True),
        name="gather",
    )(reduced)


def frames_kernel(
    range_ref, whole_ref, start_ref, end_ref, w_ref, b_ref, gain_ref, out_ref, stacked
):
    make_frames(
        lax.axis_index("seq"),
        0,
        SEQ - 2,
        range_ref,
        whole_ref,
        start_ref,
        end_ref,
        w_ref,
        b_ref,
        gain_ref,
        out_ref,
        stacked,
    )


def frames(ranges, whole, starts, ends, conv_w, conv_b, conv_gain):
    vmem = pl.BlockSpec(memory_space=pltpu.VMEM)
    return pl.pallas_call(
        frames_kernel,
        out_shape=jax.ShapeDtypeStruct((FRAMES, CHANNELS), jnp.bfloat16),
        in_specs=[pl.BlockSpec(memory_space=pltpu.SMEM)] + [vmem] * 6,
        out_specs=vmem,
        scratch_shapes=[pltpu.VMEM((FRAMES, KERNEL * CHANNELS), jnp.bfloat16)],
        compiler_params=pltpu.CompilerParams(vmem_limit_bytes=32 * MIB),
        name="frames",
    )(ranges, whole, starts, ends, conv_w, conv_b, conv_gain)


def finish_far(ranges, o, units, w_out, w_proj, starts, ends, conv_w, conv_b, conv_gain):
    whole = gather(mix(o, units, w_out, w_proj))
    return frames(ranges, whole, starts, ends, conv_w, conv_b, conv_gain)


def local(units, durations, seg_ids, ln_gain, w_qkv, w_out, w_proj, conv_w, conv_b, conv_gain):
    meta = jnp.stack([seg_ids, durations])
    kv, q, marks, seg, starts, ends, ranges = spread(
        units, ln_gain.reshape(1, WIDTH), meta, w_qkv
    )
    o = attend(ranges, kv, q, marks, seg)
    return lax.cond(
        ranges[SEQ + 8, 0] == 0,
        finish_near,
        finish_far,
        ranges,
        o,
        units,
        w_out,
        w_proj,
        starts,
        ends,
        conv_w.reshape(KERNEL * CHANNELS, CHANNELS),
        conv_b.reshape(1, CHANNELS),
        conv_gain.reshape(1, CHANNELS),
    )


def solution(mesh):
    parted = P(("grp", "seq"))
    wide = P(("grp", "seq"), None)
    return jax.shard_map(
        local,
        mesh=mesh,
        in_specs=(wide, parted, parted) + (P(),) * 7,
        out_specs=wide,
        check_vma=False,
    )
```

```python
import functools

import jax
import jax.numpy as jnp
from jax import lax
from jax.experimental import pallas as pl
from jax.experimental.pallas import tpu as pltpu
from jax.sharding import PartitionSpec as P

MESH = pl.DeviceIdType.MESH
SEQ = 32
CHIPS = 16
HEADS = 16
HEAD = 64
ROWS = 128
WIDTH = 1024
UNITS = 4096
CHANNELS = 512
KERNEL = 5
FRAMES = 768
STEP = 96
STEPS = FRAMES // STEP
TILE = 256
BLOCKS = 8
GROUPS = 8
NEG = -1e30
MIB = 1024 * 1024


def seq(index):
    return {"seq": index}


def greet(device):
    pl.semaphore_signal(
        pltpu.get_barrier_semaphore(), 1, device_id=device, device_id_type=MESH
    )


def greet_all(me):
    def one(i, carry):
        greet(seq(lax.rem(me + i, SEQ)))
        return carry

    lax.fori_loop(1, SEQ, one, 0)


def greet_row(me):
    def one(i, carry):
        greet(seq(lax.rem(me + 2 * i, SEQ)))
        return carry

    lax.fori_loop(1, CHIPS, one, 0)


def await_greetings(count):
    pl.semaphore_wait(pltpu.get_barrier_semaphore(), count)


def group_at(own, i):
    flip = own + 1 - 2 * lax.rem(own, 2)
    if i == 0:
        return flip
    if i == 1:
        return lax.rem(flip + 2, 4)
    if i == 2:
        return lax.rem(own + 2, 4)
    return own


def base_of(device):
    return jnp.clip(device - 1, 0, SEQ - 3)


def low_lanes(rows):
    return lax.broadcasted_iota(jnp.int32, (rows, 128), 1) < HEAD


def mix_kernel(
    units_ref,
    gain_ref,
    own_seg_ref,
    own_dur_ref,
    w_ref,
    w_out_ref,
    w_proj_ref,
    window_ref,
    start_ref,
    end_ref,
    range_ref,
    far_ref,
    h_ref,
    meta_ref,
    wbuf,
    send_kv,
    send_q,
    meta_all,
    flags,
    kv_ref,
    q_ref,
    mark_ref,
    seg_ref,
    even_ref,
    odd_ref,
    send_o,
    landed,
    w_out,
    w_proj,
    mine,
    w_sem,
    load_sem,
    kv_send,
    kv_recv,
    q_send,
    q_recv,
    pass_send,
    pass_recv,
    meta_send,
    meta_recv,
    flag_send,
    flag_recv,
    o_send,
    o_recv,
    near_send,
    near_recv,
    own_sem,
):
    me = lax.axis_index("seq")
    part = lax.axis_index("grp")
    core = lax.rem(me, 2)
    chip = me // 2
    sibling = me + 1 - 2 * core
    own = chip // 4
    greet_row(me)
    for there in (-1, 1):

        @pl.when((me + there >= 0) & (me + there < SEQ))
        def _():
            greet(seq(lax.rem(me + SEQ + there, SEQ)))

    def greet_part(i, carry):
        greet({"grp": lax.rem(part + i, GROUPS)})
        return carry

    lax.fori_loop(1, GROUPS, greet_part, 0)

    def w_copy(i, t):
        g = group_at(own, i)
        return pltpu.make_async_copy(
            w_ref.at[:, pl.ds(t * WIDTH + g * 256, 256)], wbuf.at[i, t], w_sem.at[i, t]
        )

    for i in range(4):
        w_copy(i, 1).start()
        w_copy(i, 2).start()
    for i in range(4):
        w_copy(i, 0).start()
    loads = [
        pltpu.make_async_copy(a, b, load_sem.at[i])
        for i, (a, b) in enumerate(((w_out_ref, w_out), (w_proj_ref, w_proj)))
    ]
    for load in loads:
        load.start()

    meta_ref[0:1, :] = own_seg_ref[...]
    meta_ref[1:2, :] = own_dur_ref[...]
    x = units_ref[...].astype(jnp.float32)
    mean = jnp.mean(x, axis=-1, keepdims=True)
    centred = x - mean
    variance = jnp.mean(centred * centred, axis=-1, keepdims=True)
    h_ref[...] = (centred / jnp.sqrt(variance + 1e-05) * gain_ref[...]).astype(jnp.bfloat16)

    def meta_copy(i, source):
        return pltpu.make_async_remote_copy(
            src_ref=meta_ref,
            dst_ref=meta_all.at[source, core],
            send_sem=meta_send.at[i],
            recv_sem=meta_recv.at[source],
            device_id=seq(lax.rem(me + 2 * i, SEQ)),
            device_id_type=MESH,
        )

    def send_meta(i, carry):
        meta_copy(i, chip).start()
        return carry

    own_meta = pltpu.make_async_copy(meta_ref, meta_all.at[chip, core], own_sem.at[2])
    pass_meta = pltpu.make_async_remote_copy(
        src_ref=meta_all.at[:, core],
        dst_ref=meta_all.at[:, core],
        send_sem=meta_send.at[0],
        recv_sem=own_sem.at[3],
        device_id=seq(sibling),
        device_id_type=MESH,
    )

    def kv_copy(head, source):
        return pltpu.make_async_remote_copy(
            src_ref=send_kv.at[head],
            dst_ref=kv_ref.at[2 * source + core],
            send_sem=kv_send.at[head],
            recv_sem=kv_recv.at[source],
            device_id=seq(2 * head + core),
            device_id_type=MESH,
        )

    def q_copy(head, source):
        return pltpu.make_async_remote_copy(
            src_ref=send_q.at[head],
            dst_ref=q_ref.at[source],
            send_sem=q_send.at[head],
            recv_sem=q_recv.at[source],
            device_id=seq(2 * head + core),
            device_id_type=MESH,
        )

    own_kv = pltpu.make_async_copy(send_kv.at[chip], kv_ref.at[me], own_sem.at[0])
    own_q = pltpu.make_async_copy(send_q.at[chip], q_ref.at[chip], own_sem.at[1])
    own_pass = pltpu.make_async_remote_copy(
        src_ref=send_kv.at[chip],
        dst_ref=kv_ref.at[me],
        send_sem=pass_send.at[chip],
        recv_sem=pass_recv.at[chip],
        device_id=seq(sibling),
        device_id_type=MESH,
    )

    low = low_lanes(ROWS // 2)
    for i in range(4):
        g = group_at(own, i)
        w_copy(i, 1).wait()
        w_copy(i, 2).wait()
        h = h_ref[...]
        k4, v4 = (
            jnp.dot(h, wbuf[i, t], preferred_element_type=jnp.float32) for t in (1, 2)
        )
        for j in range(2):
            at = slice(128 * j, 128 * j + 128)
            v2 = jnp.transpose(v4[:, at]).astype(jnp.bfloat16)
            k2 = k4[:, at]
            turned = pltpu.roll(k2, HEAD, 1)
            first = 4 * g + 2 * j
            send_kv[first, 0] = jnp.where(low, k2[:64], turned[64:]).astype(jnp.bfloat16)
            send_kv[first + 1, 0] = jnp.where(low, turned[:64], k2[64:]).astype(jnp.bfloat16)
            send_kv[first, 1] = v2[:64]
            send_kv[first + 1, 1] = v2[64:]
        if i == 0:
            beside = jnp.where(me > 0, 1, 0) + jnp.where(me < SEQ - 1, 1, 0)
            await_greetings(CHIPS - 1 + beside + GROUPS - 1)
        for r in range(4):
            if i == 3 and r == 0:
                own_kv.start()
                own_pass.start()
            else:
                kv_copy(4 * g + lax.rem(chip + r, 4), chip).start()
        if i == 0:
            lax.fori_loop(1, CHIPS, send_meta, 0)
            own_meta.start()
    for i in range(4):
        g = group_at(own, i)
        w_copy(i, 0).wait()
        q4 = jnp.dot(h_ref[...], wbuf[i, 0], preferred_element_type=jnp.float32) * 0.125
        for j in range(2):
            q2 = jnp.transpose(q4[:, 128 * j : 128 * j + 128]).astype(jnp.bfloat16)
            first = 4 * g + 2 * j
            send_q[first] = q2[:64]
            send_q[first + 1] = q2[64:]
        for r in range(4):
            if i == 3 and r == 0:
                own_q.start()
            else:
                q_copy(4 * g + lax.rem(chip + r, 4), chip).start()

    def await_meta(i, carry):
        meta_copy(i, lax.rem(chip + CHIPS - i, CHIPS)).wait()
        return carry

    lax.fori_loop(1, CHIPS, await_meta, 0)
    own_meta.wait()
    pass_meta.start()
    pass_meta.wait()
    meta = meta_all[...].reshape(SEQ, 2, 128)

    seg = meta[:, 0, :]
    dur = meta[:, 1, :].astype(jnp.float32)
    lower = (
        lax.broadcasted_iota(jnp.int32, (128, 128), 0)
        <= lax.broadcasted_iota(jnp.int32, (128, 128), 1)
    ).astype(jnp.float32).astype(jnp.bfloat16)
    earlier = (
        lax.broadcasted_iota(jnp.int32, (SEQ, SEQ), 0)
        > lax.broadcasted_iota(jnp.int32, (SEQ, SEQ), 1)
    ).astype(jnp.float32).astype(jnp.bfloat16)
    dur16 = dur.astype(jnp.bfloat16)
    within = jnp.dot(dur16, lower, preferred_element_type=jnp.float32)
    before = jnp.dot(earlier, dur16, preferred_element_type=jnp.float32)
    ends = within + jnp.sum(before, axis=1, keepdims=True)
    seg_ref[...] = seg
    start_ref[...] = (ends - dur).astype(jnp.int32)
    end_ref[...] = ends.astype(jnp.int32)

    first_frame = start_ref[:, 0:1]
    index = lax.broadcasted_iota(jnp.int32, (SEQ, 1), 0)
    late = (index >= 1) & (index <= SEQ - 3) & (first_frame > FRAMES * (index + 1) - 2)
    early = (index >= 3) & (first_frame < FRAMES * (index - 2) + FRAMES + 2)
    far = jnp.sum(jnp.where(late | early, 1.0, 0.0))
    flags[part] = jnp.zeros((8, 128), jnp.float32) + far

    def flag_copy(i, source):
        return pltpu.make_async_remote_copy(
            src_ref=flags.at[source],
            dst_ref=flags.at[source],
            send_sem=flag_send.at[i],
            recv_sem=flag_recv.at[source],
            device_id={"grp": lax.rem(part + i, GROUPS)},
            device_id_type=MESH,
        )

    def send_flag(i, carry):
        flag_copy(i, part).start()
        return carry

    lax.fori_loop(1, GROUPS, send_flag, 0)

    lane8 = lax.broadcasted_iota(jnp.int32, (8, 128), 1)
    block = jnp.zeros((8, 128), jnp.int32)
    for f in range(STEPS):
        t0 = (FRAMES * me + STEP * f - KERNEL // 2).astype(jnp.float32)
        passed = jnp.sum((ends <= t0).astype(jnp.float32)).astype(jnp.int32)
        block = jnp.where(lane8 == f, passed, block)
    range_ref[...] = block

    def mark(b, carry):
        row = jnp.broadcast_to(seg_ref[pl.ds(b, 1), :].astype(jnp.float32), (128, 128))
        column = jnp.transpose(row)
        place = lax.broadcasted_iota(jnp.int32, (64, 128), 1).astype(jnp.float32)
        marked = jnp.where(
            place < 8.0,
            jnp.where(place == column[:64], 1.0, 0.0),
            jnp.where(place == column[64:] + 8.0, 1.0, 0.0),
        )
        mark_ref[b] = marked.astype(jnp.bfloat16)
        return carry

    lax.fori_loop(0, SEQ, mark, 0)

    def await_flag(i, carry):
        flag_copy(i, lax.rem(part + GROUPS - i, GROUPS)).wait_recv()
        flag_copy(i, part).wait_send()
        return carry

    lax.fori_loop(1, GROUPS, await_flag, 0)
    total = flags[0]
    for i in range(1, GROUPS):
        total = total + flags[i]
    far_ref[0, 0] = jnp.sum(total).astype(jnp.int32)

    def passing(source):
        return pltpu.make_async_remote_copy(
            src_ref=kv_ref.at[2 * source + core],
            dst_ref=kv_ref.at[2 * source + core],
            send_sem=pass_send.at[source],
            recv_sem=pass_recv.at[source],
            device_id=seq(sibling),
            device_id_type=MESH,
        )

    for i in range(4):
        for r in range(4):
            if i == 3 and r == 0:
                continue
            source = 4 * group_at(own, i) + lax.rem(chip + 4 - r, 4)
            kv_copy(source, source).wait_recv()
            passing(source).start()

    for i in range(4):
        for r in range(4):
            source = 4 * group_at(own, i) + lax.rem(chip + 4 - r, 4)
            if i == 3 and r == 0:
                own_kv.wait()
                own_q.wait()
                own_pass.wait_recv()
            else:
                q_copy(source, source).wait_recv()
                passing(source).wait_recv()

    pairs = CHIPS // 2

    def pair_at(i):
        return lax.rem(chip // 2 + i, pairs)

    ones = jnp.ones((16, 128 * BLOCKS), jnp.bfloat16)

    def right_side(p):
        first = 4 * p + core
        q = jnp.concatenate([q_ref[2 * p], q_ref[2 * p + 1]], axis=1)
        zero = jnp.zeros((HEAD, 256), jnp.bfloat16)
        rows = lax.broadcasted_iota(jnp.int32, (8, 128), 0)
        bias = jnp.concatenate(
            [
                jnp.where(seg_ref[pl.ds(first + 2 * e, 1), :] == rows, 0.0, NEG)
                for e in range(2)
            ],
            axis=1,
        )
        none = jnp.zeros((8, 256), jnp.float32)
        biases = jnp.concatenate(
            [jnp.concatenate([bias, none], axis=0), jnp.concatenate([none, bias], axis=0)],
            axis=1,
        ).astype(jnp.bfloat16)
        return jnp.concatenate(
            [
                jnp.concatenate([q, zero], axis=1),
                jnp.concatenate([zero, q], axis=1),
                biases,
                jnp.zeros((112, 512), jnp.bfloat16),
            ],
            axis=0,
        )

    def score(right, block, keep, top):
        left = jnp.concatenate(
            [
                jnp.concatenate([kv_ref[block + t, 0], mark_ref[block + t]], axis=1)
                for t in range(BLOCKS)
            ],
            axis=0,
        )
        s = jnp.dot(left, right, preferred_element_type=jnp.float32)
        keep[...] = s
        return jnp.maximum(top, jnp.max(s.reshape(8 * BLOCKS, 8, 512), axis=0))

    def collect(top, block, kept, acc):
        w = jnp.exp(kept[...] - top).astype(jnp.bfloat16)
        w = jnp.concatenate(
            [
                w[64 * t : 64 * t + 64, 256 * h : 256 * h + 256]
                for t in range(BLOCKS)
                for h in range(2)
            ],
            axis=0,
        )
        v = jnp.concatenate([kv_ref[block + t, 1] for t in range(BLOCKS)], axis=1)
        v = jnp.concatenate([v, ones], axis=0)
        return acc + jnp.dot(v, w, preferred_element_type=jnp.float32)

    def peak(top):
        top = jnp.max(jnp.maximum(top[:, :256], top[:, 256:]), axis=0, keepdims=True)
        return jnp.concatenate([top, top], axis=1)

    def o_copy(target, source):
        return pltpu.make_async_remote_copy(
            src_ref=send_o.at[target],
            dst_ref=landed.at[source],
            send_sem=o_send.at[target],
            recv_sem=o_recv.at[source],
            device_id=seq(2 * target + core),
            device_id_type=MESH,
        )

    own_o = pltpu.make_async_copy(send_o.at[chip], landed.at[chip], own_sem.at[4])

    def give(i, acc):
        p = pair_at(i)
        out = (acc[:HEAD] / acc[HEAD : HEAD + 1]).astype(jnp.bfloat16)
        send_o[2 * p] = out[:, :128]
        send_o[2 * p + 1] = out[:, 128:]
        for e in range(2):

            @pl.when(2 * p + e != chip)
            def _():
                o_copy(2 * p + e, chip).start()

            @pl.when(2 * p + e == chip)
            def _():
                own_o.start()

    low = jnp.full((8, 512), NEG, jnp.float32)
    clear = jnp.zeros((HEAD + 16, 256), jnp.float32)
    chunks = SEQ // BLOCKS
    right = right_side(pair_at(0))
    top = low
    for n in range(chunks):
        top = score(right, BLOCKS * n, even_ref.at[n], top)

    def both(i, here, there, top):
        right = right_side(pair_at(i))
        new_top, acc = low, clear
        for n in range(chunks):
            new_top = score(right, BLOCKS * n, here.at[n], new_top)
            acc = collect(top, BLOCKS * n, there.at[n], acc)
        give(i - 1, acc)
        return peak(new_top)

    def two(i, top):
        top = both(2 * i + 1, odd_ref, even_ref, top)
        return both(2 * i + 2, even_ref, odd_ref, top)

    top = lax.fori_loop(0, pairs // 2 - 1, two, peak(top))
    top = both(pairs - 1, odd_ref, even_ref, top)
    acc = clear
    for n in range(chunks):
        acc = collect(top, BLOCKS * n, odd_ref.at[n], acc)
    give(pairs - 1, acc)

    for load in loads:
        load.wait()

    def receive(i, carry):
        o_copy(chip, lax.rem(chip + CHIPS - i, CHIPS)).wait_recv()
        return carry

    own_o.wait()
    lax.fori_loop(1, CHIPS, receive, 0)
    turned = [
        jnp.transpose(
            jnp.concatenate([landed[2 * j], landed[2 * j + 1]], axis=0).astype(jnp.float32)
        ).astype(jnp.bfloat16)
        for j in range(HEADS // 2)
    ]
    attended = jnp.concatenate(turned, axis=1)
    mixed = jnp.dot(attended, w_out[...], preferred_element_type=jnp.float32)
    mixed = (mixed + units_ref[...].astype(jnp.float32)).astype(jnp.bfloat16)
    mine[...] = jnp.dot(mixed, w_proj[...], preferred_element_type=jnp.float32).astype(
        jnp.bfloat16
    )

    def near_copy(i, target):
        slot = me - base_of(target)
        return pltpu.make_async_remote_copy(
            src_ref=mine,
            dst_ref=window_ref.at[slot],
            send_sem=near_send.at[i],
            recv_sem=near_recv.at[slot],
            device_id=seq(target),
            device_id_type=MESH,
        )

    routes = (
        (me > 0, lax.rem(me + SEQ - 1, SEQ)),
        (me < SEQ - 1, lax.rem(me + 1, SEQ)),
        (me == 2, 0),
        (me == SEQ - 3, SEQ - 1),
    )
    for i, (present, target) in enumerate(routes):

        @pl.when(present)
        def _():
            near_copy(i, target).start()

    base = base_of(me)
    own_window = pltpu.make_async_copy(mine, window_ref.at[me - base], own_sem.at[5])
    own_window.start()

    def sent(i, carry):
        o_copy(lax.rem(chip + i, CHIPS), chip).wait_send()
        return carry

    lax.fori_loop(1, CHIPS, sent, 0)
    for i in range(4):
        for r in range(4):
            source = 4 * group_at(own, i) + lax.rem(chip + 4 - r, 4)
            if i < 3 or r > 0:
                q_copy(source, source).wait_send()
                kv_copy(source, source).wait_send()
                passing(source).wait_send()
    own_pass.wait_send()

    for slot in range(3):

        @pl.when(slot != me - base)
        def _():
            pltpu.make_async_remote_copy(
                src_ref=mine,
                dst_ref=window_ref.at[slot],
                send_sem=near_send.at[0],
                recv_sem=near_recv.at[slot],
                device_id=seq(sibling),
                device_id_type=MESH,
            ).wait_recv()

    for i, (present, target) in enumerate(routes):

        @pl.when(present)
        def _():
            near_copy(i, target).wait_send()

    own_window.wait()


def mix(units, gain, seg, dur, w_qkv, w_out, w_proj):
    any_space = pl.BlockSpec(memory_space=pl.ANY)
    vmem = pl.BlockSpec(memory_space=pltpu.VMEM)
    dma = pltpu.SemaphoreType.DMA
    half = (ROWS // 2, 128)
    return pl.pallas_call(
        mix_kernel,
        out_shape=(
            jax.ShapeDtypeStruct((3, ROWS, CHANNELS), jnp.bfloat16),
            jax.ShapeDtypeStruct((SEQ, 128), jnp.int32),
            jax.ShapeDtypeStruct((SEQ, 128), jnp.int32),
            jax.ShapeDtypeStruct((8, 128), jnp.int32),
            jax.ShapeDtypeStruct((1, 1), jnp.int32),
        ),
        in_specs=[vmem] * 4 + [any_space] * 3,
        out_specs=(any_space, vmem, vmem, vmem, pl.BlockSpec(memory_space=pltpu.SMEM)),
        scratch_shapes=[
            pltpu.VMEM((ROWS, WIDTH), jnp.bfloat16),
            pltpu.VMEM((2, 128), jnp.int32),
            pltpu.VMEM((4, 3, WIDTH, 256), jnp.bfloat16),
            pltpu.VMEM((HEADS, 2) + half, jnp.bfloat16),
            pltpu.VMEM((HEADS,) + half, jnp.bfloat16),
            pltpu.VMEM((CHIPS, 2, 2, 128), jnp.int32),
            pltpu.VMEM((GROUPS, 8, 128), jnp.float32),
            pltpu.VMEM((SEQ, 2) + half, jnp.bfloat16),
            pltpu.VMEM((CHIPS,) + half, jnp.bfloat16),
            pltpu.VMEM((SEQ,) + half, jnp.bfloat16),
            pltpu.VMEM((SEQ, 128), jnp.int32),
            pltpu.VMEM((SEQ // BLOCKS, 64 * BLOCKS, 512), jnp.float32),
            pltpu.VMEM((SEQ // BLOCKS, 64 * BLOCKS, 512), jnp.float32),
            pltpu.VMEM((CHIPS,) + half, jnp.bfloat16),
            pltpu.VMEM((CHIPS,) + half, jnp.bfloat16),
            pltpu.VMEM((WIDTH, WIDTH), jnp.bfloat16),
            pltpu.VMEM((WIDTH, CHANNELS), jnp.bfloat16),
            pltpu.VMEM((ROWS, CHANNELS), jnp.bfloat16),
            dma((4, 3)),
            dma((2,)),
            dma((HEADS,)),
            dma((HEADS,)),
            dma((HEADS,)),
            dma((HEADS,)),
            dma((HEADS,)),
            dma((HEADS,)),
            dma((CHIPS,)),
            dma((CHIPS,)),
            dma((GROUPS,)),
            dma((GROUPS,)),
            dma((CHIPS,)),
            dma((CHIPS,)),
            dma((4,)),
            dma((3,)),
            dma((6,)),
        ],
        compiler_params=pltpu.CompilerParams(
            collective_id=1, has_side_effects=True, vmem_limit_bytes=56 * MIB
        ),
        name="mix",
    )(units, gain, seg, dur, w_qkv, w_out, w_proj)


def make_frames(
    me, base, last, range_ref, window_ref, start_ref, end_ref, w_ref, b_ref, gain_ref, out_ref, stacked
):
    for f in range(STEPS):
        block = jnp.clip(range_ref[0, f] // 128, base, last)
        starts = jnp.concatenate(
            [start_ref[pl.ds(block, 1), :], start_ref[pl.ds(block + 1, 1), :]], axis=1
        )
        ends = jnp.concatenate(
            [end_ref[pl.ds(block, 1), :], end_ref[pl.ds(block + 1, 1), :]], axis=1
        )
        window = window_ref[pl.ds(block - base, 2)].reshape(256, CHANNELS)
        frame = lax.broadcasted_iota(jnp.int32, (STEP, 256), 0)
        first = FRAMES * me + STEP * f - KERNEL // 2
        starts, ends = starts - first, ends - first
        for j in range(KERNEL):
            chosen = jnp.where((frame >= starts - j) & (frame < ends - j), 1.0, 0.0)
            rows = jnp.dot(
                chosen.astype(jnp.bfloat16), window, preferred_element_type=jnp.float32
            )
            stacked[STEP * f : STEP * f + STEP, CHANNELS * j : CHANNELS * j + CHANNELS] = (
                rows.astype(jnp.bfloat16)
            )
    bias, gain = b_ref[...], gain_ref[...]
    for r in range(FRAMES // TILE):
        at = slice(TILE * r, TILE * r + TILE)
        conv = jnp.dot(stacked[at, :], w_ref[...], preferred_element_type=jnp.float32) + bias
        value = jnp.maximum(conv, 0.0)
        mean = jnp.mean(value, axis=-1, keepdims=True)
        centred = value - mean
        variance = jnp.mean(centred * centred, axis=-1, keepdims=True)
        half = KERNEL // 2
        centre = stacked[at, half * CHANNELS : (half + 1) * CHANNELS].astype(jnp.float32)
        result = centre + centred / jnp.sqrt(variance + 1e-05) * gain
        out_ref[at, :] = result.astype(jnp.bfloat16)


def gather_kernel(block_ref, whole_ref, send_sem, recv_sem, own_sem):
    me = lax.axis_index("seq")
    greet_all(me)
    await_greetings(SEQ - 1)

    def copy(i, source):
        return pltpu.make_async_remote_copy(
            src_ref=block_ref,
            dst_ref=whole_ref.at[source],
            send_sem=send_sem.at[i],
            recv_sem=recv_sem.at[source],
            device_id=seq(lax.rem(me + i, SEQ)),
            device_id_type=MESH,
        )

    def send(i, carry):
        copy(i, me).start()
        return carry

    def receive(i, carry):
        copy(i, lax.rem(me + SEQ - i, SEQ)).wait()
        return carry

    lax.fori_loop(1, SEQ, send, 0)
    own = pltpu.make_async_copy(block_ref, whole_ref.at[me], own_sem)
    own.start()
    lax.fori_loop(1, SEQ, receive, 0)
    own.wait()


def gather(reduced):
    any_space = pl.BlockSpec(memory_space=pl.ANY)
    dma = pltpu.SemaphoreType.DMA
    return pl.pallas_call(
        gather_kernel,
        out_shape=jax.ShapeDtypeStruct((SEQ, ROWS, CHANNELS), jnp.bfloat16),
        in_specs=[any_space],
        out_specs=any_space,
        scratch_shapes=[dma((SEQ,)), dma((SEQ,)), dma],
        compiler_params=pltpu.CompilerParams(collective_id=4, has_side_effects=True),
        name="gather",
    )(reduced)


def frames_kernel(
    near, range_ref, rows_ref, start_ref, end_ref, w_ref, b_ref, gain_ref, out_ref, stacked
):
    me = lax.axis_index("seq")
    base = base_of(me) if near else 0
    last = base + 1 if near else SEQ - 2
    make_frames(
        me, base, last, range_ref, rows_ref, start_ref, end_ref, w_ref, b_ref, gain_ref, out_ref, stacked
    )


def frames(near, ranges, rows, starts, ends, conv_w, conv_b, conv_gain):
    vmem = pl.BlockSpec(memory_space=pltpu.VMEM)
    return pl.pallas_call(
        functools.partial(frames_kernel, near),
        out_shape=jax.ShapeDtypeStruct((FRAMES, CHANNELS), jnp.bfloat16),
        in_specs=[pl.BlockSpec(memory_space=pltpu.SMEM)] + [vmem] * 6,
        out_specs=vmem,
        scratch_shapes=[pltpu.VMEM((FRAMES, KERNEL * CHANNELS), jnp.bfloat16)],
        compiler_params=pltpu.CompilerParams(vmem_limit_bytes=60 * MIB),
        name="frames_near" if near else "frames_far",
    )(ranges, rows, starts, ends, conv_w, conv_b, conv_gain)


def finish_near(ranges, window, *rest):
    return frames(True, ranges, window, *rest)


def finish_far(ranges, window, *rest):
    me = lax.axis_index("seq")
    own = lax.dynamic_index_in_dim(window, me - base_of(me), 0, keepdims=False)
    return frames(False, ranges, gather(own), *rest)


def local(units, durations, seg_ids, ln_gain, w_qkv, w_out, w_proj, conv_w, conv_b, conv_gain):
    window, starts, ends, ranges, far = mix(
        units,
        ln_gain.reshape(1, WIDTH),
        seg_ids.reshape(1, ROWS),
        durations.reshape(1, ROWS),
        w_qkv,
        w_out,
        w_proj,
    )
    return lax.cond(
        far.reshape(()) == 0,
        finish_near,
        finish_far,
        ranges,
        window,
        starts,
        ends,
        conv_w.reshape(KERNEL * CHANNELS, CHANNELS),
        conv_b.reshape(1, CHANNELS),
        conv_gain.reshape(1, CHANNELS),
    )


def solution(mesh):
    parted = P(("grp", "seq"))
    wide = P(("grp", "seq"), None)
    return jax.shard_map(
        local,
        mesh=mesh,
        in_specs=(wide, parted, parted) + (P(),) * 7,
        out_specs=wide,
        check_vma=False,
    )
```

```python
import functools

import jax
import jax.numpy as jnp
from jax import lax
from jax.experimental import pallas as pl
from jax.experimental.pallas import tpu as pltpu
from jax.sharding import PartitionSpec as P

MESH = pl.DeviceIdType.MESH
SEQ = 32
CHIPS = 16
HEADS = 16
HEAD = 64
ROWS = 128
WIDTH = 1024
UNITS = 4096
CHANNELS = 512
KERNEL = 5
FRAMES = 768
STEP = 96
STEPS = FRAMES // STEP
TILE = 256
BLOCKS = 8
UNROLL = 2
GROUPS = 8
NEG = -1e30
MIB = 1024 * 1024


def seq(index):
    return {"seq": index}


def greet(device):
    pl.semaphore_signal(
        pltpu.get_barrier_semaphore(), 1, device_id=device, device_id_type=MESH
    )


def greet_all(me):
    def one(i, carry):
        greet(seq(lax.rem(me + i, SEQ)))
        return carry

    lax.fori_loop(1, SEQ, one, 0)


def greet_row(me):
    def one(i, carry):
        greet(seq(lax.rem(me + 2 * i, SEQ)))
        return carry

    lax.fori_loop(1, CHIPS, one, 0)


def await_greetings(count):
    pl.semaphore_wait(pltpu.get_barrier_semaphore(), count)


def group_at(own, i):
    flip = own + 1 - 2 * lax.rem(own, 2)
    if i == 0:
        return flip
    if i == 1:
        return lax.rem(flip + 2, 4)
    if i == 2:
        return lax.rem(own + 2, 4)
    return own


def base_of(device):
    return jnp.clip(device - 1, 0, SEQ - 3)


def low_lanes(rows):
    return lax.broadcasted_iota(jnp.int32, (rows, 128), 1) < HEAD


def mix_kernel(
    units_ref,
    gain_ref,
    own_seg_ref,
    own_dur_ref,
    w_ref,
    w_out_ref,
    w_proj_ref,
    window_ref,
    start_ref,
    end_ref,
    range_ref,
    far_ref,
    h_ref,
    meta_ref,
    wbuf,
    send_kq,
    send_v,
    meta_all,
    flags,
    kq_ref,
    k_ref,
    v_ref,
    mark_ref,
    seg_ref,
    scores,
    tops,
    send_o,
    landed,
    w_out,
    w_proj,
    mine,
    w_sem,
    load_sem,
    kq_send,
    kq_recv,
    v_send,
    v_recv,
    pass_k_send,
    pass_k_recv,
    pass_v_send,
    pass_v_recv,
    meta_send,
    meta_recv,
    flag_send,
    flag_recv,
    o_send,
    o_recv,
    near_send,
    near_recv,
    own_sem,
):
    me = lax.axis_index("seq")
    part = lax.axis_index("grp")
    core = lax.rem(me, 2)
    chip = me // 2
    sibling = me + 1 - 2 * core
    own = chip // 4
    greet_row(me)
    for there in (-1, 1):

        @pl.when((me + there >= 0) & (me + there < SEQ))
        def _():
            greet(seq(lax.rem(me + SEQ + there, SEQ)))

    def greet_part(i, carry):
        greet({"grp": lax.rem(part + i, GROUPS)})
        return carry

    lax.fori_loop(1, GROUPS, greet_part, 0)

    def w_copy(i, t):
        g = group_at(own, i)
        return pltpu.make_async_copy(
            w_ref.at[:, pl.ds(t * WIDTH + g * 256, 256)], wbuf.at[i, t], w_sem.at[i, t]
        )

    for i in range(4):
        w_copy(i, 0).start()
        w_copy(i, 1).start()
    for i in range(4):
        w_copy(i, 2).start()
    loads = [
        pltpu.make_async_copy(a, b, load_sem.at[i])
        for i, (a, b) in enumerate(((w_out_ref, w_out), (w_proj_ref, w_proj)))
    ]
    for load in loads:
        load.start()

    meta_ref[0:1, :] = own_seg_ref[...]
    meta_ref[1:2, :] = own_dur_ref[...]
    x = units_ref[...].astype(jnp.float32)
    mean = jnp.mean(x, axis=-1, keepdims=True)
    centred = x - mean
    variance = jnp.mean(centred * centred, axis=-1, keepdims=True)
    h_ref[...] = (centred / jnp.sqrt(variance + 1e-05) * gain_ref[...]).astype(jnp.bfloat16)

    def meta_copy(i, source):
        return pltpu.make_async_remote_copy(
            src_ref=meta_ref,
            dst_ref=meta_all.at[source, core],
            send_sem=meta_send.at[i],
            recv_sem=meta_recv.at[source],
            device_id=seq(lax.rem(me + 2 * i, SEQ)),
            device_id_type=MESH,
        )

    def send_meta(i, carry):
        meta_copy(i, chip).start()
        return carry

    own_meta = pltpu.make_async_copy(meta_ref, meta_all.at[chip, core], own_sem.at[2])
    pass_meta = pltpu.make_async_remote_copy(
        src_ref=meta_all.at[:, core],
        dst_ref=meta_all.at[:, core],
        send_sem=meta_send.at[0],
        recv_sem=own_sem.at[3],
        device_id=seq(sibling),
        device_id_type=MESH,
    )

    def kq_copy(head, source):
        return pltpu.make_async_remote_copy(
            src_ref=send_kq.at[head],
            dst_ref=kq_ref.at[source],
            send_sem=kq_send.at[head],
            recv_sem=kq_recv.at[source],
            device_id=seq(2 * head + core),
            device_id_type=MESH,
        )

    def v_copy(head, source):
        return pltpu.make_async_remote_copy(
            src_ref=send_v.at[head],
            dst_ref=v_ref.at[source, core],
            send_sem=v_send.at[head],
            recv_sem=v_recv.at[source],
            device_id=seq(2 * head + core),
            device_id_type=MESH,
        )

    def pass_k(source, block):
        return pltpu.make_async_remote_copy(
            src_ref=block,
            dst_ref=k_ref.at[source],
            send_sem=pass_k_send.at[source],
            recv_sem=pass_k_recv.at[source],
            device_id=seq(sibling),
            device_id_type=MESH,
        )

    def pass_v(source, block):
        return pltpu.make_async_remote_copy(
            src_ref=block,
            dst_ref=v_ref.at[source, core],
            send_sem=pass_v_send.at[source],
            recv_sem=pass_v_recv.at[source],
            device_id=seq(sibling),
            device_id_type=MESH,
        )

    own_kq = pltpu.make_async_copy(send_kq.at[chip], kq_ref.at[chip], own_sem.at[0])
    own_v = pltpu.make_async_copy(send_v.at[chip], v_ref.at[chip, core], own_sem.at[1])

    low = low_lanes(ROWS // 2)
    for i in range(4):
        g = group_at(own, i)
        w_copy(i, 0).wait()
        w_copy(i, 1).wait()
        h = h_ref[...]
        q4, k4 = (
            jnp.dot(h, wbuf[i, t], preferred_element_type=jnp.float32) for t in (0, 1)
        )
        for j in range(2):
            at = slice(128 * j, 128 * j + 128)
            q2 = jnp.transpose(q4[:, at] * 0.125).astype(jnp.bfloat16)
            k2 = k4[:, at]
            turned = pltpu.roll(k2, HEAD, 1)
            first = 4 * g + 2 * j
            send_kq[first, 0] = jnp.where(low, k2[:64], turned[64:]).astype(jnp.bfloat16)
            send_kq[first + 1, 0] = jnp.where(low, turned[:64], k2[64:]).astype(jnp.bfloat16)
            send_kq[first, 1] = q2[:64]
            send_kq[first + 1, 1] = q2[64:]
        if i == 0:
            beside = jnp.where(me > 0, 1, 0) + jnp.where(me < SEQ - 1, 1, 0)
            await_greetings(CHIPS - 1 + beside + GROUPS - 1)
        for r in range(4):
            if i == 3 and r == 0:
                own_kq.start()
                pass_k(chip, send_kq.at[chip, 0]).start()
            else:
                kq_copy(4 * g + lax.rem(chip + r, 4), chip).start()
        if i == 0:
            lax.fori_loop(1, CHIPS, send_meta, 0)
            own_meta.start()
    for i in range(4):
        g = group_at(own, i)
        w_copy(i, 2).wait()
        v4 = jnp.dot(h_ref[...], wbuf[i, 2], preferred_element_type=jnp.float32)
        for j in range(2):
            v2 = jnp.transpose(v4[:, 128 * j : 128 * j + 128]).astype(jnp.bfloat16)
            first = 4 * g + 2 * j
            send_v[first] = v2[:64]
            send_v[first + 1] = v2[64:]
        for r in range(4):
            if i == 3 and r == 0:
                own_v.start()
                pass_v(chip, send_v.at[chip]).start()
            else:
                v_copy(4 * g + lax.rem(chip + r, 4), chip).start()

    def await_meta(i, carry):
        meta_copy(i, lax.rem(chip + CHIPS - i, CHIPS)).wait()
        return carry

    lax.fori_loop(1, CHIPS, await_meta, 0)
    own_meta.wait()
    pass_meta.start()
    pass_meta.wait()
    meta = meta_all[...].reshape(SEQ, 2, 128)

    seg = meta[:, 0, :]
    dur = meta[:, 1, :].astype(jnp.float32)
    lower = (
        lax.broadcasted_iota(jnp.int32, (128, 128), 0)
        <= lax.broadcasted_iota(jnp.int32, (128, 128), 1)
    ).astype(jnp.float32).astype(jnp.bfloat16)
    earlier = (
        lax.broadcasted_iota(jnp.int32, (SEQ, SEQ), 0)
        > lax.broadcasted_iota(jnp.int32, (SEQ, SEQ), 1)
    ).astype(jnp.float32).astype(jnp.bfloat16)
    dur16 = dur.astype(jnp.bfloat16)
    within = jnp.dot(dur16, lower, preferred_element_type=jnp.float32)
    before = jnp.dot(earlier, dur16, preferred_element_type=jnp.float32)
    ends = within + jnp.sum(before, axis=1, keepdims=True)
    seg_ref[...] = seg
    start_ref[...] = (ends - dur).astype(jnp.int32)
    end_ref[...] = ends.astype(jnp.int32)

    first_frame = start_ref[:, 0:1]
    index = lax.broadcasted_iota(jnp.int32, (SEQ, 1), 0)
    late = (index >= 1) & (index <= SEQ - 3) & (first_frame > FRAMES * (index + 1) - 2)
    early = (index >= 3) & (first_frame < FRAMES * (index - 2) + FRAMES + 2)
    far = jnp.sum(jnp.where(late | early, 1.0, 0.0))
    flags[part] = jnp.zeros((8, 128), jnp.float32) + far

    def flag_copy(i, source):
        return pltpu.make_async_remote_copy(
            src_ref=flags.at[source],
            dst_ref=flags.at[source],
            send_sem=flag_send.at[i],
            recv_sem=flag_recv.at[source],
            device_id={"grp": lax.rem(part + i, GROUPS)},
            device_id_type=MESH,
        )

    def send_flag(i, carry):
        flag_copy(i, part).start()
        return carry

    lax.fori_loop(1, GROUPS, send_flag, 0)

    lane8 = lax.broadcasted_iota(jnp.int32, (8, 128), 1)
    block = jnp.zeros((8, 128), jnp.int32)
    for f in range(STEPS):
        t0 = (FRAMES * me + STEP * f - KERNEL // 2).astype(jnp.float32)
        passed = jnp.sum((ends <= t0).astype(jnp.float32)).astype(jnp.int32)
        block = jnp.where(lane8 == f, passed, block)
    range_ref[...] = block

    def mark(b, carry):
        row = jnp.broadcast_to(seg_ref[pl.ds(b, 1), :].astype(jnp.float32), (128, 128))
        column = jnp.transpose(row)
        place = lax.broadcasted_iota(jnp.int32, (64, 128), 1).astype(jnp.float32)
        marked = jnp.where(
            place < 8.0,
            jnp.where(place == column[:64], 1.0, 0.0),
            jnp.where(place == column[64:] + 8.0, 1.0, 0.0),
        )
        mark_ref[b] = marked.astype(jnp.bfloat16)
        return carry

    lax.fori_loop(0, SEQ, mark, 0)

    def await_flag(i, carry):
        flag_copy(i, lax.rem(part + GROUPS - i, GROUPS)).wait_recv()
        flag_copy(i, part).wait_send()
        return carry

    lax.fori_loop(1, GROUPS, await_flag, 0)
    total = flags[0]
    for i in range(1, GROUPS):
        total = total + flags[i]
    far_ref[0, 0] = jnp.sum(total).astype(jnp.int32)

    arrivals = [
        4 * group_at(own, i) + lax.rem(chip + 4 - r, 4)
        for i in range(4)
        for r in range(4)
        if i < 3 or r > 0
    ]
    for source in arrivals:
        kq_copy(source, source).wait_recv()
        pass_k(source, kq_ref.at[source, 0]).start()
    own_kq.wait()
    pass_k(chip, send_kq.at[chip, 0]).wait()
    for source in arrivals:
        pass_k(source, kq_ref.at[source, 0]).wait()

    pairs = CHIPS // 2

    def pair_at(i):
        return lax.rem(chip // 2 + i, pairs)

    ones = jnp.ones((16, 128 * BLOCKS), jnp.bfloat16)

    def right_side(p):
        first = 4 * p + core
        q = jnp.concatenate([kq_ref[2 * p, 1], kq_ref[2 * p + 1, 1]], axis=1)
        zero = jnp.zeros((HEAD, 256), jnp.bfloat16)
        rows = lax.broadcasted_iota(jnp.int32, (8, 128), 0)
        bias = jnp.concatenate(
            [
                jnp.where(seg_ref[pl.ds(first + 2 * e, 1), :] == rows, 0.0, NEG)
                for e in range(2)
            ],
            axis=1,
        )
        none = jnp.zeros((8, 256), jnp.float32)
        biases = jnp.concatenate(
            [jnp.concatenate([bias, none], axis=0), jnp.concatenate([none, bias], axis=0)],
            axis=1,
        ).astype(jnp.bfloat16)
        return jnp.concatenate(
            [
                jnp.concatenate([q, zero], axis=1),
                jnp.concatenate([zero, q], axis=1),
                biases,
                jnp.zeros((112, 512), jnp.bfloat16),
            ],
            axis=0,
        )

    def score(right, n, keep, top):
        these = range(BLOCKS // 2 * n, BLOCKS // 2 * (n + 1))
        rows = [
            jnp.concatenate([kq_ref[c, 0], mark_ref[2 * c + core]], axis=1) for c in these
        ] + [jnp.concatenate([k_ref[c], mark_ref[2 * c + 1 - core]], axis=1) for c in these]
        s = jnp.dot(
            jnp.concatenate(rows, axis=0), right, preferred_element_type=jnp.float32
        )
        keep[...] = s
        return jnp.maximum(top, jnp.max(s.reshape(8 * BLOCKS, 8, 512), axis=0))

    def collect(top, n, kept, acc):
        w = jnp.exp(kept[...] - top).astype(jnp.bfloat16)
        w = jnp.concatenate(
            [
                w[64 * t : 64 * t + 64, 256 * h : 256 * h + 256]
                for t in range(BLOCKS)
                for h in range(2)
            ],
            axis=0,
        )
        these = range(BLOCKS // 2 * n, BLOCKS // 2 * (n + 1))
        v = jnp.concatenate(
            [v_ref[c, core] for c in these] + [v_ref[c, 1 - core] for c in these], axis=1
        )
        v = jnp.concatenate([v, ones], axis=0)
        return acc + jnp.dot(v, w, preferred_element_type=jnp.float32)

    def peak(top):
        top = jnp.max(jnp.maximum(top[:, :256], top[:, 256:]), axis=0, keepdims=True)
        return jnp.concatenate([top, top], axis=1)

    def o_copy(target, source):
        return pltpu.make_async_remote_copy(
            src_ref=send_o.at[target],
            dst_ref=landed.at[source],
            send_sem=o_send.at[target],
            recv_sem=o_recv.at[source],
            device_id=seq(2 * target + core),
            device_id_type=MESH,
        )

    own_o = pltpu.make_async_copy(send_o.at[chip], landed.at[chip], own_sem.at[4])

    def give(i, acc):
        p = pair_at(i)
        out = (acc[:HEAD] / acc[HEAD : HEAD + 1]).astype(jnp.bfloat16)
        send_o[2 * p] = out[:, :128]
        send_o[2 * p + 1] = out[:, 128:]
        for e in range(2):

            @pl.when(2 * p + e != chip)
            def _():
                o_copy(2 * p + e, chip).start()

            @pl.when(2 * p + e == chip)
            def _():
                own_o.start()

    low = jnp.full((8, 512), NEG, jnp.float32)
    clear = jnp.zeros((HEAD + 16, 256), jnp.float32)
    chunks = SEQ // BLOCKS
    def score_pair(i):
        right = right_side(pair_at(i))
        top = low
        for n in range(chunks):
            top = score(right, n, scores.at[i, n], top)
        tops[i] = peak(top)

    def collect_pair(i):
        acc, top = clear, tops[i]
        for n in range(chunks):
            acc = collect(top, n, scores.at[i, n], acc)
        return acc

    for i in range(0, pairs, UNROLL):
        for u in range(UNROLL):
            score_pair(i + u)
        for source in arrivals[2 * i : 2 * (i + UNROLL)]:
            v_copy(source, source).wait_recv()
            pass_v(source, v_ref.at[source, core]).start()
    own_v.wait()
    pass_v(chip, send_v.at[chip]).wait()
    for source in arrivals:
        pass_v(source, v_ref.at[source, core]).wait()

    def some(i, carry):
        accs = [collect_pair(UNROLL * i + u) for u in range(UNROLL)]
        for u in range(UNROLL):
            give(UNROLL * i + u, accs[u])
        return carry

    lax.fori_loop(0, pairs // UNROLL, some, 0)

    for load in loads:
        load.wait()

    def receive(i, carry):
        o_copy(chip, lax.rem(chip + CHIPS - i, CHIPS)).wait_recv()
        return carry

    own_o.wait()
    lax.fori_loop(1, CHIPS, receive, 0)
    turned = [
        jnp.transpose(
            jnp.concatenate([landed[2 * j], landed[2 * j + 1]], axis=0).astype(jnp.float32)
        ).astype(jnp.bfloat16)
        for j in range(HEADS // 2)
    ]
    attended = jnp.concatenate(turned, axis=1)
    mixed = jnp.dot(attended, w_out[...], preferred_element_type=jnp.float32)
    mixed = (mixed + units_ref[...].astype(jnp.float32)).astype(jnp.bfloat16)
    mine[...] = jnp.dot(mixed, w_proj[...], preferred_element_type=jnp.float32).astype(
        jnp.bfloat16
    )

    def near_copy(i, target):
        slot = me - base_of(target)
        return pltpu.make_async_remote_copy(
            src_ref=mine,
            dst_ref=window_ref.at[slot],
            send_sem=near_send.at[i],
            recv_sem=near_recv.at[slot],
            device_id=seq(target),
            device_id_type=MESH,
        )

    routes = (
        (me > 0, lax.rem(me + SEQ - 1, SEQ)),
        (me < SEQ - 1, lax.rem(me + 1, SEQ)),
        (me == 2, 0),
        (me == SEQ - 3, SEQ - 1),
    )
    for i, (present, target) in enumerate(routes):

        @pl.when(present)
        def _():
            near_copy(i, target).start()

    base = base_of(me)
    own_window = pltpu.make_async_copy(mine, window_ref.at[me - base], own_sem.at[5])
    own_window.start()

    def sent(i, carry):
        o_copy(lax.rem(chip + i, CHIPS), chip).wait_send()
        return carry

    lax.fori_loop(1, CHIPS, sent, 0)
    for source in arrivals:
        kq_copy(source, source).wait_send()
        v_copy(source, source).wait_send()

    for slot in range(3):

        @pl.when(slot != me - base)
        def _():
            pltpu.make_async_remote_copy(
                src_ref=mine,
                dst_ref=window_ref.at[slot],
                send_sem=near_send.at[0],
                recv_sem=near_recv.at[slot],
                device_id=seq(sibling),
                device_id_type=MESH,
            ).wait_recv()

    for i, (present, target) in enumerate(routes):

        @pl.when(present)
        def _():
            near_copy(i, target).wait_send()

    own_window.wait()


def mix(units, gain, seg, dur, w_qkv, w_out, w_proj):
    any_space = pl.BlockSpec(memory_space=pl.ANY)
    vmem = pl.BlockSpec(memory_space=pltpu.VMEM)
    dma = pltpu.SemaphoreType.DMA
    half = (ROWS // 2, 128)
    return pl.pallas_call(
        mix_kernel,
        out_shape=(
            jax.ShapeDtypeStruct((3, ROWS, CHANNELS), jnp.bfloat16),
            jax.ShapeDtypeStruct((SEQ, 128), jnp.int32),
            jax.ShapeDtypeStruct((SEQ, 128), jnp.int32),
            jax.ShapeDtypeStruct((8, 128), jnp.int32),
            jax.ShapeDtypeStruct((1, 1), jnp.int32),
        ),
        in_specs=[vmem] * 4 + [any_space] * 3,
        out_specs=(any_space, vmem, vmem, vmem, pl.BlockSpec(memory_space=pltpu.SMEM)),
        scratch_shapes=[
            pltpu.VMEM((ROWS, WIDTH), jnp.bfloat16),
            pltpu.VMEM((2, 128), jnp.int32),
            pltpu.VMEM((4, 3, WIDTH, 256), jnp.bfloat16),
            pltpu.VMEM((HEADS, 2) + half, jnp.bfloat16),
            pltpu.VMEM((HEADS,) + half, jnp.bfloat16),
            pltpu.VMEM((CHIPS, 2, 2, 128), jnp.int32),
            pltpu.VMEM((GROUPS, 8, 128), jnp.float32),
            pltpu.VMEM((CHIPS, 2) + half, jnp.bfloat16),
            pltpu.VMEM((CHIPS,) + half, jnp.bfloat16),
            pltpu.VMEM((CHIPS, 2) + half, jnp.bfloat16),
            pltpu.VMEM((SEQ,) + half, jnp.bfloat16),
            pltpu.VMEM((SEQ, 128), jnp.int32),
            pltpu.VMEM((CHIPS // 2, SEQ // BLOCKS, 64 * BLOCKS, 512), jnp.float32),
            pltpu.VMEM((CHIPS // 2, 1, 512), jnp.float32),
            pltpu.VMEM((CHIPS,) + half, jnp.bfloat16),
            pltpu.VMEM((CHIPS,) + half, jnp.bfloat16),
            pltpu.VMEM((WIDTH, WIDTH), jnp.bfloat16),
            pltpu.VMEM((WIDTH, CHANNELS), jnp.bfloat16),
            pltpu.VMEM((ROWS, CHANNELS), jnp.bfloat16),
            dma((4, 3)),
            dma((2,)),
            dma((HEADS,)),
            dma((HEADS,)),
            dma((HEADS,)),
            dma((HEADS,)),
            dma((HEADS,)),
            dma((HEADS,)),
            dma((HEADS,)),
            dma((HEADS,)),
            dma((CHIPS,)),
            dma((CHIPS,)),
            dma((GROUPS,)),
            dma((GROUPS,)),
            dma((CHIPS,)),
            dma((CHIPS,)),
            dma((4,)),
            dma((3,)),
            dma((6,)),
        ],
        compiler_params=pltpu.CompilerParams(
            collective_id=1, has_side_effects=True, vmem_limit_bytes=56 * MIB
        ),
        name="mix",
    )(units, gain, seg, dur, w_qkv, w_out, w_proj)


def make_frames(
    me, base, last, range_ref, window_ref, start_ref, end_ref, w_ref, b_ref, gain_ref, out_ref, stacked
):
    for f in range(STEPS):
        block = jnp.clip(range_ref[0, f] // 128, base, last)
        starts = jnp.concatenate(
            [start_ref[pl.ds(block, 1), :], start_ref[pl.ds(block + 1, 1), :]], axis=1
        )
        ends = jnp.concatenate(
            [end_ref[pl.ds(block, 1), :], end_ref[pl.ds(block + 1, 1), :]], axis=1
        )
        window = window_ref[pl.ds(block - base, 2)].reshape(256, CHANNELS)
        frame = lax.broadcasted_iota(jnp.int32, (STEP, 256), 0)
        first = FRAMES * me + STEP * f - KERNEL // 2
        starts, ends = starts - first, ends - first
        for j in range(KERNEL):
            chosen = jnp.where((frame >= starts - j) & (frame < ends - j), 1.0, 0.0)
            rows = jnp.dot(
                chosen.astype(jnp.bfloat16), window, preferred_element_type=jnp.float32
            )
            stacked[STEP * f : STEP * f + STEP, CHANNELS * j : CHANNELS * j + CHANNELS] = (
                rows.astype(jnp.bfloat16)
            )
    bias, gain = b_ref[...], gain_ref[...]
    for r in range(FRAMES // TILE):
        at = slice(TILE * r, TILE * r + TILE)
        conv = jnp.dot(stacked[at, :], w_ref[...], preferred_element_type=jnp.float32) + bias
        value = jnp.maximum(conv, 0.0)
        mean = jnp.mean(value, axis=-1, keepdims=True)
        centred = value - mean
        variance = jnp.mean(centred * centred, axis=-1, keepdims=True)
        half = KERNEL // 2
        centre = stacked[at, half * CHANNELS : (half + 1) * CHANNELS].astype(jnp.float32)
        result = centre + centred / jnp.sqrt(variance + 1e-05) * gain
        out_ref[at, :] = result.astype(jnp.bfloat16)


def gather_kernel(block_ref, whole_ref, send_sem, recv_sem, own_sem):
    me = lax.axis_index("seq")
    greet_all(me)
    await_greetings(SEQ - 1)

    def copy(i, source):
        return pltpu.make_async_remote_copy(
            src_ref=block_ref,
            dst_ref=whole_ref.at[source],
            send_sem=send_sem.at[i],
            recv_sem=recv_sem.at[source],
            device_id=seq(lax.rem(me + i, SEQ)),
            device_id_type=MESH,
        )

    def send(i, carry):
        copy(i, me).start()
        return carry

    def receive(i, carry):
        copy(i, lax.rem(me + SEQ - i, SEQ)).wait()
        return carry

    lax.fori_loop(1, SEQ, send, 0)
    own = pltpu.make_async_copy(block_ref, whole_ref.at[me], own_sem)
    own.start()
    lax.fori_loop(1, SEQ, receive, 0)
    own.wait()


def gather(reduced):
    any_space = pl.BlockSpec(memory_space=pl.ANY)
    dma = pltpu.SemaphoreType.DMA
    return pl.pallas_call(
        gather_kernel,
        out_shape=jax.ShapeDtypeStruct((SEQ, ROWS, CHANNELS), jnp.bfloat16),
        in_specs=[any_space],
        out_specs=any_space,
        scratch_shapes=[dma((SEQ,)), dma((SEQ,)), dma],
        compiler_params=pltpu.CompilerParams(collective_id=4, has_side_effects=True),
        name="gather",
    )(reduced)


def frames_kernel(
    near, range_ref, rows_ref, start_ref, end_ref, w_ref, b_ref, gain_ref, out_ref, stacked
):
    me = lax.axis_index("seq")
    base = base_of(me) if near else 0
    last = base + 1 if near else SEQ - 2
    make_frames(
        me, base, last, range_ref, rows_ref, start_ref, end_ref, w_ref, b_ref, gain_ref, out_ref, stacked
    )


def frames(near, ranges, rows, starts, ends, conv_w, conv_b, conv_gain):
    vmem = pl.BlockSpec(memory_space=pltpu.VMEM)
    return pl.pallas_call(
        functools.partial(frames_kernel, near),
        out_shape=jax.ShapeDtypeStruct((FRAMES, CHANNELS), jnp.bfloat16),
        in_specs=[pl.BlockSpec(memory_space=pltpu.SMEM)] + [vmem] * 6,
        out_specs=vmem,
        scratch_shapes=[pltpu.VMEM((FRAMES, KERNEL * CHANNELS), jnp.bfloat16)],
        compiler_params=pltpu.CompilerParams(vmem_limit_bytes=61 * MIB),
        name="frames_near" if near else "frames_far",
    )(ranges, rows, starts, ends, conv_w, conv_b, conv_gain)


def finish_near(ranges, window, *rest):
    return frames(True, ranges, window, *rest)


def finish_far(ranges, window, *rest):
    me = lax.axis_index("seq")
    own = lax.dynamic_index_in_dim(window, me - base_of(me), 0, keepdims=False)
    return frames(False, ranges, gather(own), *rest)


def local(units, durations, seg_ids, ln_gain, w_qkv, w_out, w_proj, conv_w, conv_b, conv_gain):
    window, starts, ends, ranges, far = mix(
        units,
        ln_gain.reshape(1, WIDTH),
        seg_ids.reshape(1, ROWS),
        durations.reshape(1, ROWS),
        w_qkv,
        w_out,
        w_proj,
    )
    return lax.cond(
        far.reshape(()) == 0,
        finish_near,
        finish_far,
        ranges,
        window,
        starts,
        ends,
        conv_w.reshape(KERNEL * CHANNELS, CHANNELS),
        conv_b.reshape(1, CHANNELS),
        conv_gain.reshape(1, CHANNELS),
    )


def solution(mesh):
    parted = P(("grp", "seq"))
    wide = P(("grp", "seq"), None)
    return jax.shard_map(
        local,
        mesh=mesh,
        in_specs=(wide, parted, parted) + (P(),) * 7,
        out_specs=wide,
        check_vma=False,
    )
```

```python
import functools

import jax
import jax.numpy as jnp
from jax import lax
from jax.experimental import pallas as pl
from jax.experimental.pallas import tpu as pltpu
from jax.sharding import PartitionSpec as P

MESH = pl.DeviceIdType.MESH
SEQ = 32
CHIPS = 16
HEADS = 16
HEAD = 64
ROWS = 128
WIDTH = 1024
UNITS = 4096
CHANNELS = 512
KERNEL = 5
FRAMES = 768
STEP = 96
STEPS = FRAMES // STEP
TILE = 256
BLOCKS = 8
GROUPS = 8
NEG = -1e30
MIB = 1024 * 1024


def seq(index):
    return {"seq": index}


def greet(device):
    pl.semaphore_signal(
        pltpu.get_barrier_semaphore(), 1, device_id=device, device_id_type=MESH
    )


def greet_all(me):
    def one(i, carry):
        greet(seq(lax.rem(me + i, SEQ)))
        return carry

    lax.fori_loop(1, SEQ, one, 0)


def greet_row(me):
    def one(i, carry):
        greet(seq(lax.rem(me + 2 * i, SEQ)))
        return carry

    lax.fori_loop(1, CHIPS, one, 0)


def await_greetings(count):
    pl.semaphore_wait(pltpu.get_barrier_semaphore(), count)


def group_at(own, i):
    flip = own + 1 - 2 * lax.rem(own, 2)
    if i == 0:
        return flip
    if i == 1:
        return lax.rem(flip + 2, 4)
    if i == 2:
        return lax.rem(own + 2, 4)
    return own


def base_of(device):
    return jnp.clip(device - 1, 0, SEQ - 3)


def low_lanes(rows):
    return lax.broadcasted_iota(jnp.int32, (rows, 128), 1) < HEAD


def mix_kernel(
    units_ref,
    gain_ref,
    own_seg_ref,
    own_dur_ref,
    w_ref,
    w_out_ref,
    w_proj_ref,
    window_ref,
    start_ref,
    end_ref,
    range_ref,
    far_ref,
    h_ref,
    meta_ref,
    wbuf,
    send_kv,
    send_q,
    meta_all,
    flags,
    kv_ref,
    q_ref,
    mark_ref,
    seg_ref,
    even_ref,
    odd_ref,
    send_o,
    landed,
    w_out,
    w_proj,
    mine,
    w_sem,
    load_sem,
    kv_send,
    kv_recv,
    q_send,
    q_recv,
    pass_send,
    pass_recv,
    meta_send,
    meta_recv,
    flag_send,
    flag_recv,
    o_send,
    o_recv,
    near_send,
    near_recv,
    own_sem,
):
    me = lax.axis_index("seq")
    part = lax.axis_index("grp")
    core = lax.rem(me, 2)
    chip = me // 2
    sibling = me + 1 - 2 * core
    own = chip // 4
    def w_copy(i, t):
        g = group_at(own, i)
        return pltpu.make_async_copy(
            w_ref.at[:, pl.ds(t * WIDTH + g * 256, 256)], wbuf.at[i, t], w_sem.at[i, t]
        )

    for i in range(4):
        w_copy(i, 1).start()
        w_copy(i, 2).start()
    greet_row(me)
    for there in (-1, 1):

        @pl.when((me + there >= 0) & (me + there < SEQ))
        def _():
            greet(seq(lax.rem(me + SEQ + there, SEQ)))

    def greet_part(i, carry):
        greet({"grp": lax.rem(part + i, GROUPS)})
        return carry

    lax.fori_loop(1, GROUPS, greet_part, 0)

    for i in range(4):
        w_copy(i, 0).start()
    loads = [
        pltpu.make_async_copy(a, b, load_sem.at[i])
        for i, (a, b) in enumerate(((w_out_ref, w_out), (w_proj_ref, w_proj)))
    ]
    for load in loads:
        load.start()

    meta_ref[0:1, :] = own_seg_ref[...]
    meta_ref[1:2, :] = own_dur_ref[...]
    x = units_ref[...].astype(jnp.float32)
    mean = jnp.mean(x, axis=-1, keepdims=True)
    centred = x - mean
    variance = jnp.mean(centred * centred, axis=-1, keepdims=True)
    h_ref[...] = (centred / jnp.sqrt(variance + 1e-05) * gain_ref[...]).astype(jnp.bfloat16)

    def meta_copy(i, source):
        return pltpu.make_async_remote_copy(
            src_ref=meta_ref,
            dst_ref=meta_all.at[source, core],
            send_sem=meta_send.at[i],
            recv_sem=meta_recv.at[source],
            device_id=seq(lax.rem(me + 2 * i, SEQ)),
            device_id_type=MESH,
        )

    def send_meta(i, carry):
        meta_copy(i, chip).start()
        return carry

    own_meta = pltpu.make_async_copy(meta_ref, meta_all.at[chip, core], own_sem.at[2])
    pass_meta = pltpu.make_async_remote_copy(
        src_ref=meta_all.at[:, core],
        dst_ref=meta_all.at[:, core],
        send_sem=meta_send.at[0],
        recv_sem=own_sem.at[3],
        device_id=seq(sibling),
        device_id_type=MESH,
    )

    def kv_copy(head, source):
        return pltpu.make_async_remote_copy(
            src_ref=send_kv.at[head],
            dst_ref=kv_ref.at[2 * source + core],
            send_sem=kv_send.at[head],
            recv_sem=kv_recv.at[source],
            device_id=seq(2 * head + core),
            device_id_type=MESH,
        )

    def q_copy(head, source):
        return pltpu.make_async_remote_copy(
            src_ref=send_q.at[head],
            dst_ref=q_ref.at[source],
            send_sem=q_send.at[head],
            recv_sem=q_recv.at[source],
            device_id=seq(2 * head + core),
            device_id_type=MESH,
        )

    own_kv = pltpu.make_async_copy(send_kv.at[chip], kv_ref.at[me], own_sem.at[0])
    own_q = pltpu.make_async_copy(send_q.at[chip], q_ref.at[chip], own_sem.at[1])
    own_pass = pltpu.make_async_remote_copy(
        src_ref=send_kv.at[chip],
        dst_ref=kv_ref.at[me],
        send_sem=pass_send.at[chip],
        recv_sem=pass_recv.at[chip],
        device_id=seq(sibling),
        device_id_type=MESH,
    )

    low = low_lanes(ROWS // 2)
    for i in range(4):
        g = group_at(own, i)
        w_copy(i, 1).wait()
        w_copy(i, 2).wait()
        h = h_ref[...]
        k4, v4 = (
            jnp.dot(h, wbuf[i, t], preferred_element_type=jnp.float32) for t in (1, 2)
        )
        for j in range(2):
            at = slice(128 * j, 128 * j + 128)
            v2 = jnp.transpose(v4[:, at]).astype(jnp.bfloat16)
            k2 = k4[:, at]
            turned = pltpu.roll(k2, HEAD, 1)
            first = 4 * g + 2 * j
            send_kv[first, 0] = jnp.where(low, k2[:64], turned[64:]).astype(jnp.bfloat16)
            send_kv[first + 1, 0] = jnp.where(low, turned[:64], k2[64:]).astype(jnp.bfloat16)
            send_kv[first, 1] = v2[:64]
            send_kv[first + 1, 1] = v2[64:]
        if i == 0:
            beside = jnp.where(me > 0, 1, 0) + jnp.where(me < SEQ - 1, 1, 0)
            await_greetings(CHIPS - 1 + beside + GROUPS - 1)
        for r in range(4):
            if i == 3 and r == 0:
                own_kv.start()
                own_pass.start()
            else:
                kv_copy(4 * g + lax.rem(chip + r, 4), chip).start()
        if i == 0:
            lax.fori_loop(1, CHIPS, send_meta, 0)
            own_meta.start()
    for i in range(4):
        g = group_at(own, i)
        w_copy(i, 0).wait()
        q4 = jnp.dot(h_ref[...], wbuf[i, 0], preferred_element_type=jnp.float32) * 0.125
        for j in range(2):
            q2 = jnp.transpose(q4[:, 128 * j : 128 * j + 128]).astype(jnp.bfloat16)
            first = 4 * g + 2 * j
            send_q[first] = q2[:64]
            send_q[first + 1] = q2[64:]

    own_q.start()
    beside_chip = chip + 1 - 2 * lax.rem(chip, 2)
    pairs = CHIPS // 2
    q_targets = [beside_chip] + [
        2 * lax.rem(chip // 2 + pairs - i, pairs) + e for i in range(1, pairs) for e in range(2)
    ]
    for target in q_targets:
        q_copy(target, chip).start()

    def await_meta(i, carry):
        meta_copy(i, lax.rem(chip + CHIPS - i, CHIPS)).wait()
        return carry

    lax.fori_loop(1, CHIPS, await_meta, 0)
    own_meta.wait()
    pass_meta.start()
    pass_meta.wait()
    meta = meta_all[...].reshape(SEQ, 2, 128)

    seg = meta[:, 0, :]
    dur = meta[:, 1, :].astype(jnp.float32)
    lower = (
        lax.broadcasted_iota(jnp.int32, (128, 128), 0)
        <= lax.broadcasted_iota(jnp.int32, (128, 128), 1)
    ).astype(jnp.float32).astype(jnp.bfloat16)
    earlier = (
        lax.broadcasted_iota(jnp.int32, (SEQ, SEQ), 0)
        > lax.broadcasted_iota(jnp.int32, (SEQ, SEQ), 1)
    ).astype(jnp.float32).astype(jnp.bfloat16)
    dur16 = dur.astype(jnp.bfloat16)
    within = jnp.dot(dur16, lower, preferred_element_type=jnp.float32)
    before = jnp.dot(earlier, dur16, preferred_element_type=jnp.float32)
    ends = within + jnp.sum(before, axis=1, keepdims=True)
    seg_ref[...] = seg
    start_ref[...] = (ends - dur).astype(jnp.int32)
    end_ref[...] = ends.astype(jnp.int32)

    first_frame = start_ref[:, 0:1]
    index = lax.broadcasted_iota(jnp.int32, (SEQ, 1), 0)
    late = (index >= 1) & (index <= SEQ - 3) & (first_frame > FRAMES * (index + 1) - 2)
    early = (index >= 3) & (first_frame < FRAMES * (index - 2) + FRAMES + 2)
    far = jnp.sum(jnp.where(late | early, 1.0, 0.0))
    flags[part] = jnp.zeros((8, 128), jnp.float32) + far

    def flag_copy(i, source):
        return pltpu.make_async_remote_copy(
            src_ref=flags.at[source],
            dst_ref=flags.at[source],
            send_sem=flag_send.at[i],
            recv_sem=flag_recv.at[source],
            device_id={"grp": lax.rem(part + i, GROUPS)},
            device_id_type=MESH,
        )

    def send_flag(i, carry):
        flag_copy(i, part).start()
        return carry

    lax.fori_loop(1, GROUPS, send_flag, 0)

    lane8 = lax.broadcasted_iota(jnp.int32, (8, 128), 1)
    block = jnp.zeros((8, 128), jnp.int32)
    for f in range(STEPS):
        t0 = (FRAMES * me + STEP * f - KERNEL // 2).astype(jnp.float32)
        passed = jnp.sum((ends <= t0).astype(jnp.float32)).astype(jnp.int32)
        block = jnp.where(lane8 == f, passed, block)
    range_ref[...] = block

    def mark(b, carry):
        row = jnp.broadcast_to(seg_ref[pl.ds(b, 1), :].astype(jnp.float32), (128, 128))
        column = jnp.transpose(row)
        place = lax.broadcasted_iota(jnp.int32, (64, 128), 1).astype(jnp.float32)
        marked = jnp.where(
            place < 8.0,
            jnp.where(place == column[:64], 1.0, 0.0),
            jnp.where(place == column[64:] + 8.0, 1.0, 0.0),
        )
        mark_ref[b] = marked.astype(jnp.bfloat16)
        return carry

    lax.fori_loop(0, SEQ, mark, 0)

    def await_flag(i, carry):
        flag_copy(i, lax.rem(part + GROUPS - i, GROUPS)).wait_recv()
        flag_copy(i, part).wait_send()
        return carry

    lax.fori_loop(1, GROUPS, await_flag, 0)
    total = flags[0]
    for i in range(1, GROUPS):
        total = total + flags[i]
    far_ref[0, 0] = jnp.sum(total).astype(jnp.int32)

    def passing(source):
        return pltpu.make_async_remote_copy(
            src_ref=kv_ref.at[2 * source + core],
            dst_ref=kv_ref.at[2 * source + core],
            send_sem=pass_send.at[source],
            recv_sem=pass_recv.at[source],
            device_id=seq(sibling),
            device_id_type=MESH,
        )

    arrivals = [
        4 * group_at(own, i) + lax.rem(chip + 4 - r, 4)
        for i in range(4)
        for r in range(4)
        if i < 3 or r > 0
    ]
    for j, source in enumerate(arrivals):
        kv_copy(source, source).wait_recv()
        passing(source).start()

    own_kv.wait()
    own_pass.wait_recv()
    for source in arrivals:
        passing(source).wait_recv()


    def pair_at(i):
        return lax.rem(chip // 2 + i, pairs)

    ones = jnp.ones((16, 128 * BLOCKS), jnp.bfloat16)

    def right_side(p):
        first = 4 * p + core
        q = jnp.concatenate([q_ref[2 * p], q_ref[2 * p + 1]], axis=1)
        zero = jnp.zeros((HEAD, 256), jnp.bfloat16)
        rows = lax.broadcasted_iota(jnp.int32, (8, 128), 0)
        bias = jnp.concatenate(
            [
                jnp.where(seg_ref[pl.ds(first + 2 * e, 1), :] == rows, 0.0, NEG)
                for e in range(2)
            ],
            axis=1,
        )
        none = jnp.zeros((8, 256), jnp.float32)
        biases = jnp.concatenate(
            [jnp.concatenate([bias, none], axis=0), jnp.concatenate([none, bias], axis=0)],
            axis=1,
        ).astype(jnp.bfloat16)
        return jnp.concatenate(
            [
                jnp.concatenate([q, zero], axis=1),
                jnp.concatenate([zero, q], axis=1),
                biases,
                jnp.zeros((112, 512), jnp.bfloat16),
            ],
            axis=0,
        )

    def score(right, block, keep, top):
        left = jnp.concatenate(
            [
                jnp.concatenate([kv_ref[block + t, 0], mark_ref[block + t]], axis=1)
                for t in range(BLOCKS)
            ],
            axis=0,
        )
        s = jnp.dot(left, right, preferred_element_type=jnp.float32)
        keep[...] = s
        return jnp.maximum(top, jnp.max(s.reshape(8 * BLOCKS, 8, 512), axis=0))

    def collect(top, block, kept, acc):
        w = jnp.exp(kept[...] - top).astype(jnp.bfloat16)
        w = jnp.concatenate(
            [
                w[64 * t : 64 * t + 64, 256 * h : 256 * h + 256]
                for t in range(BLOCKS)
                for h in range(2)
            ],
            axis=0,
        )
        v = jnp.concatenate([kv_ref[block + t, 1] for t in range(BLOCKS)], axis=1)
        v = jnp.concatenate([v, ones], axis=0)
        return acc + jnp.dot(v, w, preferred_element_type=jnp.float32)

    def peak(top):
        top = jnp.max(jnp.maximum(top[:, :256], top[:, 256:]), axis=0, keepdims=True)
        return jnp.concatenate([top, top], axis=1)

    def o_copy(target, source):
        return pltpu.make_async_remote_copy(
            src_ref=send_o.at[target],
            dst_ref=landed.at[source],
            send_sem=o_send.at[target],
            recv_sem=o_recv.at[source],
            device_id=seq(2 * target + core),
            device_id_type=MESH,
        )

    own_o = pltpu.make_async_copy(send_o.at[chip], landed.at[chip], own_sem.at[4])

    def give(i, acc):
        p = pair_at(i)
        out = (acc[:HEAD] / acc[HEAD : HEAD + 1]).astype(jnp.bfloat16)
        send_o[2 * p] = out[:, :128]
        send_o[2 * p + 1] = out[:, 128:]
        for e in range(2):

            @pl.when(2 * p + e != chip)
            def _():
                o_copy(2 * p + e, chip).start()

            @pl.when(2 * p + e == chip)
            def _():
                own_o.start()

    low = jnp.full((8, 512), NEG, jnp.float32)
    clear = jnp.zeros((HEAD + 16, 256), jnp.float32)
    chunks = SEQ // BLOCKS
    own_q.wait()
    q_copy(beside_chip, beside_chip).wait_recv()
    right = right_side(pair_at(0))
    top = low
    for n in range(chunks):
        top = score(right, BLOCKS * n, even_ref.at[n], top)

    def both(i, here, there, top):
        for e in range(2):
            source = 2 * pair_at(i) + e
            q_copy(source, source).wait_recv()
        right = right_side(pair_at(i))
        new_top, acc = low, clear
        for n in range(chunks):
            new_top = score(right, BLOCKS * n, here.at[n], new_top)
            acc = collect(top, BLOCKS * n, there.at[n], acc)
        give(i - 1, acc)
        return peak(new_top)

    def two(i, top):
        top = both(2 * i + 1, odd_ref, even_ref, top)
        return both(2 * i + 2, even_ref, odd_ref, top)

    top = lax.fori_loop(0, pairs // 2 - 1, two, peak(top))
    top = both(pairs - 1, odd_ref, even_ref, top)
    acc = clear
    for n in range(chunks):
        acc = collect(top, BLOCKS * n, odd_ref.at[n], acc)
    give(pairs - 1, acc)

    for load in loads:
        load.wait()

    mixed = jnp.zeros((ROWS, WIDTH), jnp.float32)
    for i in range(pairs):
        p = lax.rem(chip // 2 + pairs - i, pairs)
        if i == 0:
            own_o.wait()
            o_copy(chip, beside_chip).wait_recv()
        else:
            for e in range(2):
                o_copy(chip, 2 * p + e).wait_recv()
        heads = landed[pl.ds(2 * p, 2)].reshape(128, 128)
        turned = jnp.transpose(heads.astype(jnp.float32)).astype(jnp.bfloat16)
        rows = w_out[pl.ds(pl.multiple_of(128 * p, 128), 128), :]
        mixed = mixed + jnp.dot(turned, rows, preferred_element_type=jnp.float32)
    mixed = (mixed + units_ref[...].astype(jnp.float32)).astype(jnp.bfloat16)
    mine[...] = jnp.dot(mixed, w_proj[...], preferred_element_type=jnp.float32).astype(
        jnp.bfloat16
    )

    def near_copy(i, target):
        slot = me - base_of(target)
        return pltpu.make_async_remote_copy(
            src_ref=mine,
            dst_ref=window_ref.at[slot],
            send_sem=near_send.at[i],
            recv_sem=near_recv.at[slot],
            device_id=seq(target),
            device_id_type=MESH,
        )

    routes = (
        (me > 0, lax.rem(me + SEQ - 1, SEQ)),
        (me < SEQ - 1, lax.rem(me + 1, SEQ)),
        (me == 2, 0),
        (me == SEQ - 3, SEQ - 1),
    )
    for i, (present, target) in enumerate(routes):

        @pl.when(present)
        def _():
            near_copy(i, target).start()

    base = base_of(me)
    own_window = pltpu.make_async_copy(mine, window_ref.at[me - base], own_sem.at[5])
    own_window.start()

    def sent(i, carry):
        o_copy(lax.rem(chip + i, CHIPS), chip).wait_send()
        return carry

    lax.fori_loop(1, CHIPS, sent, 0)
    for source in arrivals:
        q_copy(source, source).wait_send()
        kv_copy(source, source).wait_send()
        passing(source).wait_send()
    own_pass.wait_send()

    for slot in range(3):

        @pl.when(slot != me - base)
        def _():
            pltpu.make_async_remote_copy(
                src_ref=mine,
                dst_ref=window_ref.at[slot],
                send_sem=near_send.at[0],
                recv_sem=near_recv.at[slot],
                device_id=seq(sibling),
                device_id_type=MESH,
            ).wait_recv()

    for i, (present, target) in enumerate(routes):

        @pl.when(present)
        def _():
            near_copy(i, target).wait_send()

    own_window.wait()


def mix(units, gain, seg, dur, w_qkv, w_out, w_proj):
    any_space = pl.BlockSpec(memory_space=pl.ANY)
    vmem = pl.BlockSpec(memory_space=pltpu.VMEM)
    dma = pltpu.SemaphoreType.DMA
    half = (ROWS // 2, 128)
    return pl.pallas_call(
        mix_kernel,
        out_shape=(
            jax.ShapeDtypeStruct((3, ROWS, CHANNELS), jnp.bfloat16),
            jax.ShapeDtypeStruct((SEQ, 128), jnp.int32),
            jax.ShapeDtypeStruct((SEQ, 128), jnp.int32),
            jax.ShapeDtypeStruct((8, 128), jnp.int32),
            jax.ShapeDtypeStruct((1, 1), jnp.int32),
        ),
        in_specs=[vmem] * 4 + [any_space] * 3,
        out_specs=(any_space, vmem, vmem, vmem, pl.BlockSpec(memory_space=pltpu.SMEM)),
        scratch_shapes=[
            pltpu.VMEM((ROWS, WIDTH), jnp.bfloat16),
            pltpu.VMEM((2, 128), jnp.int32),
            pltpu.VMEM((4, 3, WIDTH, 256), jnp.bfloat16),
            pltpu.VMEM((HEADS, 2) + half, jnp.bfloat16),
            pltpu.VMEM((HEADS,) + half, jnp.bfloat16),
            pltpu.VMEM((CHIPS, 2, 2, 128), jnp.int32),
            pltpu.VMEM((GROUPS, 8, 128), jnp.float32),
            pltpu.VMEM((SEQ, 2) + half, jnp.bfloat16),
            pltpu.VMEM((CHIPS,) + half, jnp.bfloat16),
            pltpu.VMEM((SEQ,) + half, jnp.bfloat16),
            pltpu.VMEM((SEQ, 128), jnp.int32),
            pltpu.VMEM((SEQ // BLOCKS, 64 * BLOCKS, 512), jnp.float32),
            pltpu.VMEM((SEQ // BLOCKS, 64 * BLOCKS, 512), jnp.float32),
            pltpu.VMEM((CHIPS,) + half, jnp.bfloat16),
            pltpu.VMEM((CHIPS,) + half, jnp.bfloat16),
            pltpu.VMEM((WIDTH, WIDTH), jnp.bfloat16),
            pltpu.VMEM((WIDTH, CHANNELS), jnp.bfloat16),
            pltpu.VMEM((ROWS, CHANNELS), jnp.bfloat16),
            dma((4, 3)),
            dma((2,)),
            dma((HEADS,)),
            dma((HEADS,)),
            dma((HEADS,)),
            dma((HEADS,)),
            dma((HEADS,)),
            dma((HEADS,)),
            dma((CHIPS,)),
            dma((CHIPS,)),
            dma((GROUPS,)),
            dma((GROUPS,)),
            dma((CHIPS,)),
            dma((CHIPS,)),
            dma((4,)),
            dma((3,)),
            dma((6,)),
        ],
        compiler_params=pltpu.CompilerParams(
            collective_id=1, has_side_effects=True, vmem_limit_bytes=56 * MIB
        ),
        name="mix",
    )(units, gain, seg, dur, w_qkv, w_out, w_proj)


def make_frames(
    me, base, last, range_ref, window_ref, start_ref, end_ref, w_ref, b_ref, gain_ref, out_ref, stacked
):
    for f in range(STEPS):
        block = jnp.clip(range_ref[0, f] // 128, base, last)
        starts = jnp.concatenate(
            [start_ref[pl.ds(block, 1), :], start_ref[pl.ds(block + 1, 1), :]], axis=1
        )
        ends = jnp.concatenate(
            [end_ref[pl.ds(block, 1), :], end_ref[pl.ds(block + 1, 1), :]], axis=1
        )
        window = window_ref[pl.ds(block - base, 2)].reshape(256, CHANNELS)
        frame = lax.broadcasted_iota(jnp.int32, (STEP, 256), 0)
        first = FRAMES * me + STEP * f - KERNEL // 2
        starts, ends = starts - first, ends - first
        chosen = jnp.concatenate(
            [
                jnp.where((frame >= starts - j) & (frame < ends - j), 1.0, 0.0).astype(jnp.bfloat16)
                for j in range(KERNEL)
            ],
            axis=0,
        )
        rows = jnp.dot(chosen, window, preferred_element_type=jnp.float32).astype(jnp.bfloat16)
        for j in range(KERNEL):
            stacked[STEP * f : STEP * f + STEP, CHANNELS * j : CHANNELS * j + CHANNELS] = rows[
                STEP * j : STEP * j + STEP
            ]
    bias, gain = b_ref[...], gain_ref[...]
    for r in range(FRAMES // TILE):
        at = slice(TILE * r, TILE * r + TILE)
        conv = jnp.dot(stacked[at, :], w_ref[...], preferred_element_type=jnp.float32) + bias
        value = jnp.maximum(conv, 0.0)
        mean = jnp.mean(value, axis=-1, keepdims=True)
        centred = value - mean
        variance = jnp.mean(centred * centred, axis=-1, keepdims=True)
        half = KERNEL // 2
        centre = stacked[at, half * CHANNELS : (half + 1) * CHANNELS].astype(jnp.float32)
        result = centre + centred / jnp.sqrt(variance + 1e-05) * gain
        out_ref[at, :] = result.astype(jnp.bfloat16)


def gather_kernel(block_ref, whole_ref, send_sem, recv_sem, own_sem):
    me = lax.axis_index("seq")
    greet_all(me)
    await_greetings(SEQ - 1)

    def copy(i, source):
        return pltpu.make_async_remote_copy(
            src_ref=block_ref,
            dst_ref=whole_ref.at[source],
            send_sem=send_sem.at[i],
            recv_sem=recv_sem.at[source],
            device_id=seq(lax.rem(me + i, SEQ)),
            device_id_type=MESH,
        )

    def send(i, carry):
        copy(i, me).start()
        return carry

    def receive(i, carry):
        copy(i, lax.rem(me + SEQ - i, SEQ)).wait()
        return carry

    lax.fori_loop(1, SEQ, send, 0)
    own = pltpu.make_async_copy(block_ref, whole_ref.at[me], own_sem)
    own.start()
    lax.fori_loop(1, SEQ, receive, 0)
    own.wait()


def gather(reduced):
    any_space = pl.BlockSpec(memory_space=pl.ANY)
    dma = pltpu.SemaphoreType.DMA
    return pl.pallas_call(
        gather_kernel,
        out_shape=jax.ShapeDtypeStruct((SEQ, ROWS, CHANNELS), jnp.bfloat16),
        in_specs=[any_space],
        out_specs=any_space,
        scratch_shapes=[dma((SEQ,)), dma((SEQ,)), dma],
        compiler_params=pltpu.CompilerParams(collective_id=4, has_side_effects=True),
        name="gather",
    )(reduced)


def frames_kernel(
    near, range_ref, rows_ref, start_ref, end_ref, w_ref, b_ref, gain_ref, out_ref, stacked
):
    me = lax.axis_index("seq")
    base = base_of(me) if near else 0
    last = base + 1 if near else SEQ - 2
    make_frames(
        me, base, last, range_ref, rows_ref, start_ref, end_ref, w_ref, b_ref, gain_ref, out_ref, stacked
    )


def frames(near, ranges, rows, starts, ends, conv_w, conv_b, conv_gain):
    vmem = pl.BlockSpec(memory_space=pltpu.VMEM)
    return pl.pallas_call(
        functools.partial(frames_kernel, near),
        out_shape=jax.ShapeDtypeStruct((FRAMES, CHANNELS), jnp.bfloat16),
        in_specs=[pl.BlockSpec(memory_space=pltpu.SMEM)] + [vmem] * 6,
        out_specs=vmem,
        scratch_shapes=[pltpu.VMEM((FRAMES, KERNEL * CHANNELS), jnp.bfloat16)],
        compiler_params=pltpu.CompilerParams(vmem_limit_bytes=61 * MIB),
        name="frames_near" if near else "frames_far",
    )(ranges, rows, starts, ends, conv_w, conv_b, conv_gain)


def finish_near(ranges, window, *rest):
    return frames(True, ranges, window, *rest)


def finish_far(ranges, window, *rest):
    me = lax.axis_index("seq")
    own = lax.dynamic_index_in_dim(window, me - base_of(me), 0, keepdims=False)
    return frames(False, ranges, gather(own), *rest)


def local(units, durations, seg_ids, ln_gain, w_qkv, w_out, w_proj, conv_w, conv_b, conv_gain):
    window, starts, ends, ranges, far = mix(
        units,
        ln_gain.reshape(1, WIDTH),
        seg_ids.reshape(1, ROWS),
        durations.reshape(1, ROWS),
        w_qkv,
        w_out,
        w_proj,
    )
    return lax.cond(
        far.reshape(()) == 0,
        finish_near,
        finish_far,
        ranges,
        window,
        starts,
        ends,
        conv_w.reshape(KERNEL * CHANNELS, CHANNELS),
        conv_b.reshape(1, CHANNELS),
        conv_gain.reshape(1, CHANNELS),
    )


def solution(mesh):
    parted = P(("grp", "seq"))
    wide = P(("grp", "seq"), None)
    return jax.shard_map(
        local,
        mesh=mesh,
        in_specs=(wide, parted, parted) + (P(),) * 7,
        out_specs=wide,
        check_vma=False,
    )
```
